32 devices in a mesh: dp: 8 (over z, core), shard: 4 (over y, x).
Axes of the slice: x: 2, y: 2, z: 4, core: 2. Of those that a mesh axis runs over, the one named last changes fastest.
Arguments:
- queries: float32 [16384, 256], P(('dp', 'shard'))
- items: float32 [81920, 256], P('shard')
- positive: int32 [16384], P(('dp', 'shard')), may hold values from 0 to 81919
- tile_ids: int32 [32, 4, 3], P(('dp', 'shard')), may hold values from 0 to 39, as said below
- counts: int32 [32, 4], P(('dp', 'shard')), may hold values from 1 to 3, as said below
Outputs:
- loss: float32 [16384], P(('dp', 'shard'))
- query_grad: float32 [16384, 256], P(('dp', 'shard'))
- item_grad: float32 [81920, 256], P(('shard', 'dp'))
The draws below stay inside these ranges and needn't reach their ends.
Inputs may be any that keep to these rules, and one draw needn't show every extreme that they name: `tile_ids`: within one block and shard the 3 entries are distinct; only the first counts of them are visited. `counts`: every block visits exactly 3 tiles on at least one shard.
All inputs are finite; a program needn't handle non-finite values.
Results may differ from the reference program's by a relative error of at most 0.0003.
Values sent between devices are 32-bit elements; how exact they have to be, the bound alone decides.
No kernel may reach another device: no remote copies, remote signals or barrier semaphores. Data moves between devices by JAX's collectives and lax.ppermute only.
A program may use at most 192 MiB of HBM per device.

```python
import jax
import jax.numpy as jnp
from jax import lax

D = 256
TILE = 512
TILES_DEV = 40
QDEV = 512
KMAX = 3
BLOCKS = 32
QUERIES = 16384
ITEMS = 81920
N_SHARD = 4


def shared_items(key):
    return jax.random.normal(jax.random.fold_in(key, 5), (ITEMS, D), jnp.float32)


def shared_positive(key):
    return jax.random.randint(jax.random.fold_in(key, 11), (QUERIES,), 0, ITEMS, dtype=jnp.int32)


def shared_tile_ids(key):
    scores = jax.random.randint(jax.random.fold_in(key, 21), (BLOCKS, N_SHARD, TILES_DEV), 0, 1048576, dtype=jnp.int32)
    scores = scores * TILES_DEV + jnp.arange(TILES_DEV, dtype=jnp.int32)
    order = jnp.argsort(scores, axis=-1, stable=True)
    return order[:, :, :KMAX].astype(jnp.int32)


def draw_items(key, part):
    return shared_items(key)


def draw_positive(key, part):
    return shared_positive(key)


def draw_tile_ids(key, part):
    return shared_tile_ids(key)


def draw_queries(key, part):
    base = jax.random.normal(jax.random.fold_in(key, 3), (QUERIES, D), jnp.float32) * 0.0625
    table = shared_items(key)
    pos_id = shared_positive(key)
    row_ids = jnp.arange(QUERIES, dtype=jnp.int32)
    first_tile = shared_tile_ids(key)[row_ids // QDEV, 0, 0]
    cand_id = first_tile * TILE + row_ids % TILE
    other_id = first_tile * TILE + (row_ids + 1) % TILE
    cand_id = jnp.where(cand_id == pos_id, other_id, cand_id)
    pos_vec = table[pos_id]
    cand_vec = table[cand_id]
    pp = jnp.sum(pos_vec * pos_vec, axis=1)
    pc = jnp.sum(pos_vec * cand_vec, axis=1)
    cc = jnp.sum(cand_vec * cand_vec, axis=1)
    level = jax.random.uniform(jax.random.fold_in(key, 4), (QUERIES,), jnp.float32, 110.0, 300.0)
    gap = jax.random.uniform(jax.random.fold_in(key, 7), (QUERIES,), jnp.float32, 1.0, 3.0)
    second = level - gap
    det = pp * cc - pc * pc
    coef_p = (level * cc - second * pc) / det
    coef_c = (second * pp - level * pc) / det
    aligned = coef_p[:, None] * pos_vec + coef_c[:, None] * cand_vec
    picked = (row_ids % 64 == 0)[:, None]
    return jnp.where(picked, aligned, base)


def draw_counts(key, part):
    heavy = jax.random.randint(jax.random.fold_in(key, 31), (BLOCKS, 1), 0, N_SHARD, dtype=jnp.int32)
    lighter = jax.random.randint(jax.random.fold_in(key, 32), (BLOCKS, N_SHARD), 1, KMAX, dtype=jnp.int32)
    return jnp.where(jnp.arange(N_SHARD, dtype=jnp.int32)[None, :] == heavy, KMAX, lighter).astype(jnp.int32)


def setup_inputs(seed: int = 0) -> dict:
    seeds = jax.random.split(jax.random.key(seed), 6)
    return {
        "queries": draw_queries(jax.random.fold_in(seeds[5], 71), 0),
        "items": draw_items(jax.random.fold_in(seeds[5], 71), 0),
        "positive": draw_positive(jax.random.fold_in(seeds[5], 71), 0),
        "tile_ids": draw_tile_ids(jax.random.fold_in(seeds[5], 71), 0),
        "counts": draw_counts(jax.random.fold_in(seeds[5], 71), 0),
    }


very_low = -1.0e30


def reference(queries, items, positive, tile_ids, counts):
    blocks = QUERIES // QDEV
    local_rows = TILES_DEV * TILE
    query_blocks = queries.reshape(blocks, QDEV, D)
    pos_blocks = positive.reshape(blocks, QDEV)
    high = lax.Precision.HIGHEST

    def one_block(grads, xs):
        qblk, pblk, ids, cnt = xs
        starts = jnp.arange(N_SHARD, dtype=jnp.int32)[:, None] * local_rows + ids * TILE
        row_index = (starts[:, :, None] + jnp.arange(TILE, dtype=jnp.int32)[None, None, :]).reshape(-1)
        live = jnp.arange(KMAX, dtype=jnp.int32)[None, :] < cnt[:, None]
        live = jnp.broadcast_to(live[:, :, None], (N_SHARD, KMAX, TILE)).reshape(-1)
        cand = items[row_index]
        logits = jnp.dot(qblk, cand.T, precision=high, preferred_element_type=jnp.float32)
        logits = jnp.where(live[None, :], logits, very_low)
        chosen = items[pblk]
        plogit = jnp.sum(qblk * chosen, axis=1)
        top = jnp.maximum(jnp.max(logits, axis=1), plogit)
        total = jnp.sum(jnp.where(live[None, :], jnp.exp(logits - top[:, None]), 0.0), axis=1) + jnp.exp(plogit - top)
        lse = top + jnp.log(total)
        loss = lse - plogit
        prob = jnp.where(live[None, :], jnp.exp(logits - lse[:, None]), 0.0)
        weight = jnp.exp(plogit - lse) - 1.0
        dq = jnp.dot(prob, cand, precision=high, preferred_element_type=jnp.float32) + weight[:, None] * chosen
        grads = grads.at[row_index].add(jnp.dot(prob.T, qblk, precision=high, preferred_element_type=jnp.float32))
        grads = grads.at[pblk].add(weight[:, None] * qblk)
        return grads, (loss, dq)

    start = jnp.zeros((ITEMS, D), jnp.float32)
    grads, (loss, dq) = lax.scan(one_block, start, (query_blocks, pos_blocks, tile_ids, counts))
    return loss.reshape(QUERIES), dq.reshape(QUERIES, D), grads
```

```python
import functools

import jax
import jax.numpy as jnp
from jax import lax
from jax.experimental import pallas as pl
from jax.experimental.pallas import tpu as pltpu
from jax.sharding import PartitionSpec as P

TILE = 512
KMAX = 3
EXTRA = 8
MIB = 1024 * 1024

very_low = -1e30
high, highest = lax.Precision.HIGH, lax.Precision.HIGHEST


def dot(a, b, dims=((1,), (0,)), precision=high):
    return lax.dot_general(a, b, (dims, ((), ())), precision=precision, preferred_element_type=jnp.float32)


def pack_kernel(q_ref, row_ref, col_ref, lists_ref, out_ref):
    rows, width = q_ref.shape
    out_ref[:rows, :] = q_ref[...]
    out_ref[rows : rows + EXTRA, :] = jnp.zeros((EXTRA, width), jnp.float32)
    row, col = row_ref[...], col_ref[...]
    at_row = lax.broadcasted_iota(jnp.int32, (rows, rows), 1)
    at_col = lax.broadcasted_iota(jnp.int32, (rows, rows), 0)
    before = (row < col) | ((row == col) & (at_row < at_col))
    rank = jnp.sum(before.astype(jnp.float32), axis=1, keepdims=True)
    placed = rank == at_row.astype(jnp.float32)
    sorted_pos = jnp.sum(jnp.where(placed, col, 0.0), axis=0, keepdims=True)
    sorted_at = jnp.sum(jnp.where(placed, at_col.astype(jnp.float32), 0.0), axis=0, keepdims=True)
    per = rows // width
    for first, values in ((0, row), (per, sorted_pos), (2 * per, sorted_at)):
        for i in range(per):
            out_ref[rows + first + i : rows + first + i + 1, :] = values[:, i * width : (i + 1) * width]
    out_ref[rows + 3 * per : rows + 3 * per + 1, :] = lists_ref[...]


def pack(queries, positive, tile_ids, counts):
    rows, width = queries.shape
    lists = jnp.concatenate([tile_ids.reshape(-1), counts.reshape(-1)]).astype(jnp.float32)
    lists = jnp.pad(lists, (0, width - lists.shape[0])).reshape(1, width)
    pos = positive.astype(jnp.float32)
    return pl.pallas_call(
        pack_kernel,
        out_shape=jax.ShapeDtypeStruct((rows + EXTRA, width), jnp.float32),
        compiler_params=pltpu.CompilerParams(vmem_limit_bytes=24 * MIB),
        name="pack",
    )(queries, pos.reshape(1, rows), pos.reshape(rows, 1), lists)


def unpack(messages, shard_at, n_shard):
    rows, width = messages[0].shape[0] - EXTRA, messages[0].shape[1]
    per = rows // width
    meta = jnp.stack([m[rows:] for m in messages]).astype(jnp.int32)
    n = len(messages)
    pos = meta[:, :per].reshape(n, rows)
    sorted_pos = meta[:, per : 2 * per].reshape(n, rows)
    places = meta[:, 2 * per : 3 * per].reshape(n, rows)
    lists = meta[:, 3 * per]
    ids = lists[:, : n_shard * KMAX].reshape(n, n_shard, KMAX)
    cnt = lists[:, n_shard * KMAX : n_shard * (KMAX + 1)]
    ids = lax.dynamic_index_in_dim(ids, shard_at, 1, False)
    cnt = lax.dynamic_index_in_dim(cnt, shard_at, 1, False)
    return pos, sorted_pos, places, ids, cnt


def span(sorted_pos, start, length):
    return jnp.stack([jnp.sum(sorted_pos < start, axis=1), jnp.sum(sorted_pos < start + length, axis=1)], axis=1).astype(jnp.int32)


def swap(x, axis, bits):
    return lax.ppermute(x, axis, [(i, i ^ bits) for i in range(lax.axis_size(axis))])


def plane(message, half):
    n = lax.axis_size("shard")
    slots = [message]
    for j in range(1, n):
        top_bit, low_bit = 1 << (j.bit_length() - 1), j & -j
        if j == top_bit:
            slots.append(swap(message, "shard", j))
        else:
            first = swap(slots[j ^ top_bit][:half], "shard", top_bit)
            second = swap(slots[j ^ low_bit][half:], "shard", low_bit)
            slots.append((first, second))
            slots[j] = jnp.concatenate(slots[j], axis=0)
    return slots


def stats_kernel(n, base, ids, cnt, sorted_pos, places, where, *refs):
    msgs = refs[:n]
    pos_ref, items_hbm, acc_ref, chosen_ref, stat_ref, q_ref, tiles, items, rowbuf, sems = refs[n:]
    rows = q_ref.shape[1]
    local_rows = items.shape[0]
    for j in range(n):
        pltpu.make_async_copy(msgs[j].at[:rows], q_ref.at[j], sems.at[0, j]).start()

    def tile_copy(b, k):
        return pltpu.make_async_copy(
            items_hbm.at[pl.ds(pl.multiple_of(ids[b, k] * TILE, TILE), TILE)], tiles.at[b * KMAX + k], sems.at[1, b * KMAX + k]
        )

    for b in range(n):
        for k in range(KMAX):

            @pl.when(k < cnt[b])
            def _():
                tile_copy(b, k).start()

    whole = pltpu.make_async_copy(items_hbm, items, sems.at[2, 0])
    whole.start()
    for j in range(n):
        pltpu.make_async_copy(msgs[j].at[:rows], q_ref.at[j], sems.at[0, j]).wait()

    @pl.loop(0, n)
    def _(b):
        q_t = q_ref[b].T
        acc_ref[b] = jnp.zeros(acc_ref.shape[1:], jnp.float32)

        def visit(k, carry):
            top, total = carry
            tile_copy(b, k).wait()
            tile = tiles[b * KMAX + k]
            logits = dot(tile, q_t, precision=highest)
            new_top = jnp.maximum(top, jnp.max(logits, axis=0, keepdims=True))
            prob = jnp.exp(logits - new_top)
            scale = jnp.exp(top - new_top)
            total = total * scale + jnp.sum(prob, axis=0, keepdims=True)
            acc_ref[b] = acc_ref[b] * scale + dot(tile.T, prob)
            return new_top, total

        start = (jnp.full((1, rows), very_low, jnp.float32), jnp.zeros((1, rows), jnp.float32))
        top, total = lax.fori_loop(0, cnt[b], visit, start)
        stat_ref[b, 0:1, :] = top
        stat_ref[b, 1:2, :] = total

    whole.wait()

    @pl.loop(0, n)
    def _(b):
        rowbuf[...] = jnp.zeros(rowbuf.shape, jnp.float32)

        @pl.loop(where[b, 0], where[b, 1])
        def _(i):
            rowbuf[pl.ds(places[b, i], 1), :] = items[pl.ds(sorted_pos[b, i] - base[0], 1), :]

        chosen = rowbuf[...].T
        chosen_ref[b] = chosen
        offset = pos_ref[pl.ds(b, 1), :] - base[0]
        inside = (offset >= 0) & (offset < local_rows)
        plogit = jnp.sum(q_ref[b].T * chosen, axis=0, keepdims=True)
        top, total = stat_ref[b, 0:1, :], stat_ref[b, 1:2, :]
        new_top = jnp.maximum(top, jnp.where(inside, plogit, very_low))
        total = total * jnp.exp(top - new_top) + jnp.where(inside, jnp.exp(plogit - new_top), 0.0)
        stat_ref[b, 1:2, :] = new_top + jnp.log(total)
        stat_ref[b, 2:3, :] = jnp.where(inside, plogit, 0.0)
        stat_ref[b, 3:4, :] = jnp.where(inside, 1.0, 0.0)
        stat_ref[b, 4:8, :] = jnp.zeros((4, rows), jnp.float32)


def stats(messages, meta, items, base):
    n = len(messages)
    rows, width = messages[0].shape[0] - EXTRA, messages[0].shape[1]
    pos, sorted_pos, places, ids, cnt = meta
    smem, hbm = pl.BlockSpec(memory_space=pltpu.SMEM), pl.BlockSpec(memory_space=pl.ANY)
    vmem = pl.BlockSpec(memory_space=pltpu.VMEM)
    return pl.pallas_call(
        functools.partial(stats_kernel, n),
        out_shape=(
            jax.ShapeDtypeStruct((n, width, rows), jnp.float32),
            jax.ShapeDtypeStruct((n, width, rows), jnp.float32),
            jax.ShapeDtypeStruct((n, 8, rows), jnp.float32),
        ),
        in_specs=[smem] * 6 + [hbm] * n + [vmem, hbm],
        out_specs=(vmem, vmem, vmem),
        scratch_shapes=[
            pltpu.VMEM((n, rows, width), jnp.float32),
            pltpu.VMEM((n * KMAX, TILE, width), jnp.float32),
            pltpu.VMEM(items.shape, jnp.float32),
            pltpu.VMEM((rows, width), jnp.float32),
            pltpu.SemaphoreType.DMA((3, n * KMAX)),
        ],
        compiler_params=pltpu.CompilerParams(vmem_limit_bytes=56 * MIB),
        name="stats",
    )(base, ids, cnt, sorted_pos, places, span(sorted_pos, base[0], items.shape[0]), *messages, pos, items)


def dq_kernel(acc_ref, chosen_ref, stat_ref, lse_ref, plog_ref, first_ref, second_ref):
    n, _, rows = acc_ref.shape
    half = rows // 2

    @pl.loop(0, n)
    def _(b):
        lse = lse_ref[pl.ds(b, 1), :]
        weight = (jnp.exp(plog_ref[pl.ds(b, 1), :] - lse) - 1.0) * stat_ref[b, 3:4, :]
        d = (acc_ref[b] * jnp.exp(stat_ref[b, 0:1, :] - lse) + chosen_ref[b] * weight).T
        first_ref[b] = d[:half]
        second_ref[b] = d[half:]


def dq_shares(acc, chosen, stat, lse, plog):
    n, width, rows = acc.shape
    out = jax.ShapeDtypeStruct((n, rows // 2, width), jnp.float32)
    return pl.pallas_call(
        dq_kernel, out_shape=(out, out), compiler_params=pltpu.CompilerParams(vmem_limit_bytes=32 * MIB), name="dq"
    )(acc, chosen, stat, lse, plog)


def reduce_slots(shares, order):
    slots = {j: shares[j] for j in range(shares.shape[0])}
    for bit in order:
        out = [j for j in sorted(slots) if j & bit]
        got = swap(jnp.stack([slots[j] for j in out]), "shard", bit)
        slots = {j ^ bit: slots[j ^ bit] + got[i] for i, j in enumerate(out)}
    return slots[0]


def item_kernel(n, base, ids, cnt, sorted_pos, places, where, weight, *refs):
    msgs = refs[:n]
    lse_ref, items_hbm, acc_hbm, out_hbm, q_ref, items, acc, sems = refs[n:]
    rows = q_ref.shape[1]
    span_rows = acc.shape[0]
    tiles = span_rows // TILE
    get_acc = pltpu.make_async_copy(acc_hbm, acc, sems.at[n])
    get_acc.start()
    get_items = pltpu.make_async_copy(
        items_hbm.at[pl.ds(pl.multiple_of(base[1] * TILE, TILE), span_rows)], items, sems.at[n + 1]
    )
    get_items.start()
    for j in range(n):
        pltpu.make_async_copy(msgs[j].at[:rows], q_ref.at[j], sems.at[j]).start()
    get_acc.wait()
    get_items.wait()
    for j in range(n):
        pltpu.make_async_copy(msgs[j].at[:rows], q_ref.at[j], sems.at[j]).wait()

    @pl.loop(0, n)
    def _(b):
        @pl.loop(0, cnt[b])
        def _(k):
            tile = ids[b, k] - base[1]

            @pl.when((tile >= 0) & (tile < tiles))
            def _():
                at = pl.ds(pl.multiple_of(tile * TILE, TILE), TILE)
                q = q_ref[b]
                logits = dot(items[at, :], q, ((1,), (1,)), highest)
                prob = jnp.exp(logits - lse_ref[pl.ds(b, 1), :])
                acc[at, :] += dot(prob, q)

        @pl.loop(where[b, 0], where[b, 1])
        def _(i):
            place = places[b, i]
            at = pl.ds(sorted_pos[b, i] - base[0], 1)
            acc[at, :] += q_ref[b, pl.ds(place, 1), :] * weight[b, place]

    put = pltpu.make_async_copy(acc, out_hbm, sems.at[n])
    put.start()
    put.wait()


def item_grads(messages, meta, lse, weight, items, acc, base):
    n = len(messages)
    rows, width = messages[0].shape[0] - EXTRA, messages[0].shape[1]
    _, sorted_pos, places, ids, cnt = meta
    smem, hbm = pl.BlockSpec(memory_space=pltpu.SMEM), pl.BlockSpec(memory_space=pl.ANY)
    vmem = pl.BlockSpec(memory_space=pltpu.VMEM)
    return pl.pallas_call(
        functools.partial(item_kernel, n),
        out_shape=jax.ShapeDtypeStruct(acc.shape, jnp.float32),
        in_specs=[smem] * 7 + [hbm] * n + [vmem, hbm, hbm],
        out_specs=hbm,
        scratch_shapes=[
            pltpu.VMEM((n, rows, width), jnp.float32),
            pltpu.VMEM(acc.shape, jnp.float32),
            pltpu.VMEM(acc.shape, jnp.float32),
            pltpu.SemaphoreType.DMA((n + 2,)),
        ],
        input_output_aliases={7 + n + 2: 0},
        compiler_params=pltpu.CompilerParams(vmem_limit_bytes=32 * MIB),
        name="item_grads",
    )(base, ids, cnt, sorted_pos, places, span(sorted_pos, base[0], acc.shape[0]), weight, *messages, lse, items, acc)


def local(queries, items, positive, tile_ids, counts):
    dp_at, shard_at = lax.axis_index("dp"), lax.axis_index("shard")
    n_dp, n_shard = lax.axis_size("dp"), lax.axis_size("shard")
    rows, width = queries.shape
    local_rows = items.shape[0]
    own_rows = local_rows // n_dp
    half = rows // 2

    message = pack(queries, positive, tile_ids, counts)
    far = [message] + [swap(message, "dp", 2 * k) for k in range(1, n_dp // 2)]
    group = plane(message, half)
    groups = [group] + [plane(m, half) for m in far[1:]]
    metas = [unpack(g, shard_at, n_shard) for g in groups]

    item_base = (shard_at * local_rows).astype(jnp.int32)
    acc, chosen, stat = stats(group, metas[0], items, item_base.reshape(1))

    parts = stat[:, 1:3]
    bit = 1
    while bit < n_shard:
        got = swap(parts, "shard", bit)
        got = got[jnp.array([j ^ bit for j in range(n_shard)])]
        top = jnp.maximum(parts[:, 0], got[:, 0])
        lse = top + jnp.log(jnp.exp(parts[:, 0] - top) + jnp.exp(got[:, 0] - top))
        parts = jnp.stack([lse, parts[:, 1] + got[:, 1]], axis=1)
        bit *= 2
    lse, plog = parts[:, 0], parts[:, 1]
    loss = lse[0] - plog[0]

    first, second = dq_shares(acc, chosen, stat, lse, plog)
    bits = [1 << i for i in range(n_shard.bit_length() - 1)]
    query_grad = jnp.concatenate([reduce_slots(first, bits), reduce_slots(second, bits[::-1])], axis=0)

    pair_rows = 2 * own_rows
    pair_at = dp_at // 2
    base = jnp.stack([item_base + pair_at * pair_rows, pair_at * pair_rows // TILE]).astype(jnp.int32)
    weight = jnp.exp(plog - lse) - 1.0
    sent = jnp.stack([lse, weight], axis=1)
    terms = [sent] + [swap(sent, "dp", 2 * k) for k in range(1, n_dp // 2)]
    grads = jnp.zeros((pair_rows, width), jnp.float32)
    for g, meta, term in zip(groups, metas, terms):
        grads = item_grads(g, meta, term[:, 0], term[:, 1], items, grads, base)
    core = dp_at % 2
    mine = lax.dynamic_slice_in_dim(grads, core * own_rows, own_rows, 0)
    other = lax.dynamic_slice_in_dim(grads, (1 - core) * own_rows, own_rows, 0)
    item_grad = mine + swap(other, "dp", 1)
    return loss, query_grad, item_grad


def solution(mesh):
    placed = (
        P(("dp", "shard"), None),
        P("shard", None),
        P(("dp", "shard")),
        P(("dp", "shard"), None, None),
        P(("dp", "shard"), None),
    )
    return jax.shard_map(
        local,
        mesh=mesh,
        in_specs=placed,
        out_specs=(P(("dp", "shard")), P(("dp", "shard"), None), P(("shard", "dp"), None)),
        check_vma=False,
    )
```

```python
import functools

import jax
import jax.numpy as jnp
from jax import lax
from jax.experimental import pallas as pl
from jax.experimental.pallas import tpu as pltpu
from jax.sharding import PartitionSpec as P

TILE = 512
KMAX = 3
EXTRA = 8
STAT = 4
MIB = 1024 * 1024

very_low = -1e30
high, highest = lax.Precision.HIGH, lax.Precision.HIGHEST

smem = pl.BlockSpec(memory_space=pltpu.SMEM)
vmem = pl.BlockSpec(memory_space=pltpu.VMEM)
anywhere = pl.BlockSpec(memory_space=pl.ANY)


def dot(a, b, dims=((1,), (0,)), precision=high):
    return lax.dot_general(a, b, (dims, ((), ())), precision=precision, preferred_element_type=jnp.float32)


def cost(us):
    return pl.CostEstimate(flops=0, bytes_accessed=int(us * 3.0e6), transcendentals=0)


def pack_kernel(q_ref, pos_ref, lists_ref, out_ref):
    rows, width = q_ref.shape
    out_ref[:rows, :] = q_ref[...]
    out_ref[rows : rows + EXTRA, :] = jnp.zeros((EXTRA, width), jnp.float32)
    row = pos_ref[...].astype(jnp.float32)
    col = jnp.broadcast_to(row, (8, rows)).T[:, 0:1]
    at_row = lax.broadcasted_iota(jnp.int32, (rows, rows), 1)
    at_col = lax.broadcasted_iota(jnp.int32, (rows, rows), 0)
    before = (row < col) | ((row == col) & (at_row < at_col))
    rank = jnp.sum(before.astype(jnp.float32), axis=1, keepdims=True)
    placed = rank == at_row.astype(jnp.float32)
    sorted_pos = jnp.sum(jnp.where(placed, col, 0.0), axis=0, keepdims=True)
    sorted_at = jnp.sum(jnp.where(placed, at_col.astype(jnp.float32), 0.0), axis=0, keepdims=True)
    per = rows // width
    for first, values in ((0, row), (per, sorted_pos), (2 * per, sorted_at)):
        for i in range(per):
            out_ref[rows + first + i : rows + first + i + 1, :] = values[:, i * width : (i + 1) * width]
    out_ref[rows + 3 * per : rows + 3 * per + 1, :] = lists_ref[...].astype(jnp.float32)


def pack(queries, positive, tile_ids, counts):
    rows, width = queries.shape
    lists = jnp.concatenate([tile_ids.reshape(-1), counts.reshape(-1)])
    lists = jnp.pad(lists, (0, width - lists.shape[0])).reshape(1, width)
    return pl.pallas_call(
        pack_kernel,
        out_shape=jax.ShapeDtypeStruct((rows + EXTRA, width), jnp.float32),
        compiler_params=pltpu.CompilerParams(vmem_limit_bytes=24 * MIB),
        cost_estimate=cost(2),
        name="pack",
    )(queries, positive.reshape(1, rows), lists)


class Lists:
    def __init__(self, ref, rows, shard_at, n_shard):
        self.ref, self.rows, self.shard_at, self.n_shard = ref, rows, shard_at, n_shard
        self.width = ref.shape[2]
        self.per = rows // self.width
        self.shift = self.width.bit_length() - 1

    def entry(self, b, first, i):
        return self.ref[b, first + (i >> self.shift), i & (self.width - 1)]

    def sorted_pos(self, b, i):
        return self.entry(b, self.per, i).astype(jnp.int32)

    def place(self, b, i):
        return self.entry(b, 2 * self.per, i).astype(jnp.int32)

    def tile(self, b, k):
        return self.ref[b, 3 * self.per, self.shard_at * KMAX + k].astype(jnp.int32)

    def count(self, b):
        return self.ref[b, 3 * self.per, self.n_shard * KMAX + self.shard_at].astype(jnp.int32)

    def first_from(self, b, start):
        def halve(_, ends):
            low, top = ends
            mid = (low + top) >> 1
            below = (low < top) & (self.sorted_pos(b, jnp.minimum(mid, self.rows - 1)) < start)
            return jnp.where(below, mid + 1, low), jnp.where(below | (low >= top), top, mid)

        return lax.fori_loop(0, self.rows.bit_length(), halve, (jnp.int32(0), jnp.int32(self.rows)))[0]


def swap(x, axis, bits):
    return lax.ppermute(x, axis, [(i, i ^ bits) for i in range(lax.axis_size(axis))])


def after(x, *others):
    return lax.optimization_barrier((x, *others))[0]


def plane(message, by_top):
    slots = [message]
    for j in range(1, lax.axis_size("shard")):
        bit = 1 << (j.bit_length() - 1) if by_top else j & -j
        slots.append(swap(slots[j ^ bit], "shard", bit))
    return slots


def stats_kernel(n, n_before, n_shard, at, *refs):
    msgs, refs = refs[:n], refs[n:]
    befores, refs = refs[:n_before], refs[n_before:]
    items_hbm, acc_ref, chosen_ref, stat_ref, q_ref, tiles, rowbuf, lists_ref, sems, row_sems = refs
    rows = q_ref.shape[1] - EXTRA
    width = q_ref.shape[2]
    per = rows // width
    lists = Lists(lists_ref, rows, at[0], n_shard)
    base, local_rows = at[1], items_hbm.shape[0]

    def get_lists(j):
        return pltpu.make_async_copy(msgs[j].at[rows : rows + EXTRA], lists_ref.at[j], sems.at[0, j])

    def get_q(j):
        return pltpu.make_async_copy(msgs[j], q_ref.at[j], sems.at[1, j])

    def get_tile(b, k):
        start = pl.multiple_of(lists.tile(b, k) * TILE, TILE)
        return pltpu.make_async_copy(items_hbm.at[pl.ds(start, TILE)], tiles.at[b * KMAX + k], sems.at[2 + k, b])

    def get_row(b, i):
        return pltpu.make_async_copy(
            items_hbm.at[pl.ds(lists.sorted_pos(b, i) - base, 1)], rowbuf.at[b, pl.ds(lists.place(b, i), 1)], row_sems.at[b]
        )

    for j in range(n):
        get_lists(j).start()
    for j in range(n):
        get_q(j).start()
    first = 0
    for before in befores:
        stat_ref[first : first + before.shape[0]] = before[...]
        first += before.shape[0]
    rowbuf[...] = jnp.zeros(rowbuf.shape, jnp.float32)
    for j in range(n):
        get_lists(j).wait()

    @pl.loop(0, n)
    def _(b):
        @pl.loop(0, lists.count(b))
        def _(k):
            get_tile(b, k).start()

    spans = []
    for b in range(n):
        spans.append((lists.first_from(b, base), lists.first_from(b, base + local_rows)))

        @pl.loop(*spans[b])
        def _(i):
            get_row(b, i).start()

    for j in range(n):
        get_q(j).wait()

    @pl.loop(0, n)
    def _(b):
        q_t = q_ref[b, :rows, :].T
        acc_ref[b] = jnp.zeros(acc_ref.shape[1:], jnp.float32)

        def visit(k, carry):
            top, total = carry
            get_tile(b, k).wait()
            tile = tiles[b * KMAX + k]
            logits = dot(tile, q_t, precision=highest)
            new_top = jnp.maximum(top, jnp.max(logits, axis=0, keepdims=True))
            prob = jnp.exp(logits - new_top)
            scale = jnp.exp(top - new_top)
            total = total * scale + jnp.sum(prob, axis=0, keepdims=True)
            acc_ref[b] = acc_ref[b] * scale + dot(tile.T, prob)
            return new_top, total

        start = (jnp.full((1, rows), very_low, jnp.float32), jnp.zeros((1, rows), jnp.float32))
        top, total = lax.fori_loop(0, lists.count(b), visit, start)
        stat_ref[first + b, 0:1, :] = top
        stat_ref[first + b, 1:2, :] = total

    for b in range(n):

        @pl.loop(*spans[b])
        def _(i):
            get_row(b, i).wait()

    @pl.loop(0, n)
    def _(b):
        chosen = rowbuf[b].T
        chosen_ref[b] = chosen
        pos = jnp.concatenate([q_ref[b, rows + i : rows + i + 1, :] for i in range(per)], axis=1).astype(jnp.int32)
        offset = pos - base
        inside = (offset >= 0) & (offset < local_rows)
        plogit = jnp.sum(q_ref[b, :rows, :].T * chosen, axis=0, keepdims=True)
        top, total = stat_ref[first + b, 0:1, :], stat_ref[first + b, 1:2, :]
        new_top = jnp.maximum(top, jnp.where(inside, plogit, very_low))
        total = total * jnp.exp(top - new_top) + jnp.where(inside, jnp.exp(plogit - new_top), 0.0)
        stat_ref[first + b, 1:2, :] = new_top + jnp.log(total)
        stat_ref[first + b, 2:3, :] = jnp.where(inside, plogit, 0.0)
        stat_ref[first + b, 3:4, :] = jnp.where(inside, 1.0, 0.0)


def stats(messages, befores, items, at):
    n = len(messages)
    rows, width = messages[0].shape[0] - EXTRA, messages[0].shape[1]
    total = n + sum(b.shape[0] for b in befores)
    sums = jax.ShapeDtypeStruct((n, width, rows), jnp.float32)
    return pl.pallas_call(
        functools.partial(stats_kernel, n, len(befores), lax.axis_size("shard")),
        out_shape=(sums, sums, jax.ShapeDtypeStruct((total, STAT, rows), jnp.float32)),
        in_specs=[smem] + [anywhere] * n + [vmem] * len(befores) + [anywhere],
        out_specs=(vmem, vmem, vmem),
        scratch_shapes=[
            pltpu.VMEM((n, rows + EXTRA, width), jnp.float32),
            pltpu.VMEM((n * KMAX, TILE, width), jnp.float32),
            pltpu.VMEM((n, rows, width), jnp.float32),
            pltpu.SMEM((n, EXTRA, width), jnp.float32),
            pltpu.SemaphoreType.DMA((2 + KMAX, n)),
            pltpu.SemaphoreType.DMA((n,)),
        ],
        compiler_params=pltpu.CompilerParams(vmem_limit_bytes=40 * MIB),
        cost_estimate=cost(5 * n),
        name="stats",
    )(at, *messages, *befores, items)


def dq_kernel(n, counts, *refs):
    stat_refs, refs = refs[:n], refs[n:]
    acc_refs, refs = refs[: len(counts)], refs[len(counts) :]
    chosen_refs, refs = refs[: len(counts)], refs[len(counts) :]
    loss_ref, term_ref, share_refs = refs[0], refs[1], refs[2:]
    b = 0
    for acc_ref, chosen_ref, count in zip(acc_refs, chosen_refs, counts):
        for i in range(count):
            parts = [stat_refs[j][b ^ j, 1:2, :] for j in range(n)]
            top = functools.reduce(jnp.maximum, parts)
            lse = top + jnp.log(sum(jnp.exp(p - top) for p in parts))
            plogit = sum(stat_refs[j][b ^ j, 2:3, :] for j in range(n))
            weight = jnp.exp(plogit - lse) - 1.0
            term_ref[0, b : b + 1, :] = lse
            term_ref[1, b : b + 1, :] = weight
            if b == 0:
                loss_ref[...] = lse - plogit
            own = stat_refs[0]
            share = acc_ref[i] * jnp.exp(own[b, 0:1, :] - lse) + chosen_ref[i] * (weight * own[b, 3:4, :])
            share_refs[b][...] = share.T
            b += 1


def dq_shares(all_stats, accs, chosens):
    n, _, rows = all_stats[0].shape
    width = accs[0].shape[1]
    share = jax.ShapeDtypeStruct((rows, width), jnp.float32)
    out = pl.pallas_call(
        functools.partial(dq_kernel, n, [a.shape[0] for a in accs]),
        out_shape=(
            jax.ShapeDtypeStruct((1, rows), jnp.float32),
            jax.ShapeDtypeStruct((2, n, rows), jnp.float32),
            *[share] * n,
        ),
        compiler_params=pltpu.CompilerParams(vmem_limit_bytes=40 * MIB),
        cost_estimate=cost(3),
        name="dq",
    )(*all_stats, *accs, *chosens)
    return out[0], out[1], out[2:]


def item_kernel(n, n_shard, is_first, is_last, at, weight, *refs):
    msgs, refs = refs[:n], refs[n:]
    lse_ref, items_hbm, refs = refs[0], refs[1], refs[2:]
    if not is_first:
        acc_hbm, refs = refs[0], refs[1:]
    outs, refs = refs[: 1 + is_last], refs[1 + is_last :]
    q_ref, items, acc, lists_ref, sems = refs
    rows, width = q_ref.shape[1], q_ref.shape[2]
    span_rows = acc.shape[0]
    tiles = span_rows // TILE
    base, first_tile, core = at[1] + at[2] * TILE, at[2], at[3]
    lists = Lists(lists_ref, rows, at[0], n_shard)
    start = pl.multiple_of(first_tile * TILE, TILE)
    get_items = pltpu.make_async_copy(items_hbm.at[pl.ds(start, span_rows)], items, sems.at[2, 0])

    def get_lists(j):
        return pltpu.make_async_copy(msgs[j].at[rows : rows + EXTRA], lists_ref.at[j], sems.at[0, j])

    def get_q(j):
        return pltpu.make_async_copy(msgs[j].at[:rows], q_ref.at[j], sems.at[1, j])

    for j in range(n):
        get_lists(j).start()
    if is_first:
        get_items.start()
        acc[...] = jnp.zeros(acc.shape, jnp.float32)
    else:
        get_acc = pltpu.make_async_copy(acc_hbm, acc, sems.at[2, 1])
        get_acc.start()
        get_items.start()
    for j in range(n):
        get_q(j).start()
    for j in range(n):
        get_lists(j).wait()
    if not is_first:
        get_acc.wait()
    for j in range(n):
        get_q(j).wait()

    @pl.loop(0, n)
    def _(b):
        @pl.loop(lists.first_from(b, base), lists.first_from(b, base + span_rows))
        def _(i):
            place = lists.place(b, i)
            here = pl.ds(lists.sorted_pos(b, i) - base, 1)
            acc[here, :] += q_ref[b, pl.ds(place, 1), :] * weight[1, b, place]

    get_items.wait()

    @pl.loop(0, n)
    def _(b):
        @pl.loop(0, lists.count(b))
        def _(k):
            tile = lists.tile(b, k) - first_tile

            @pl.when((tile >= 0) & (tile < tiles))
            def _():
                here = pl.ds(pl.multiple_of(tile * TILE, TILE), TILE)
                q = q_ref[b]
                logits = dot(items[here, :], q, ((1,), (1,)), highest)
                prob = jnp.exp(logits - lse_ref[0, pl.ds(b, 1), :])
                acc[here, :] += dot(prob, q)

    if is_last:
        own = span_rows // 2
        mine, other = outs
        put = [
            pltpu.make_async_copy(acc.at[pl.ds(pl.multiple_of((1 - core) * own, 8), own)], other, sems.at[2, 0]),
            pltpu.make_async_copy(acc.at[pl.ds(pl.multiple_of(core * own, 8), own)], mine, sems.at[2, 1]),
        ]
    else:
        put = [pltpu.make_async_copy(acc, outs[0], sems.at[2, 0])]
    for p in put:
        p.start()
    for p in put:
        p.wait()


def item_grads(messages, terms, items, acc, span_rows, at, is_last):
    n = len(messages)
    rows, width = messages[0].shape[0] - EXTRA, messages[0].shape[1]
    is_first = acc is None
    half = jax.ShapeDtypeStruct((span_rows // 2, width), jnp.float32)
    whole = jax.ShapeDtypeStruct((span_rows, width), jnp.float32)
    carried = [] if is_first else [acc]
    return pl.pallas_call(
        functools.partial(item_kernel, n, lax.axis_size("shard"), is_first, is_last),
        out_shape=(half, half) if is_last else whole,
        in_specs=[smem] * 2 + [anywhere] * n + [vmem, anywhere] + [anywhere] * len(carried),
        out_specs=(anywhere, anywhere) if is_last else anywhere,
        scratch_shapes=[
            pltpu.VMEM((n, rows, width), jnp.float32),
            pltpu.VMEM((span_rows, width), jnp.float32),
            pltpu.VMEM((span_rows, width), jnp.float32),
            pltpu.SMEM((n, EXTRA, width), jnp.float32),
            pltpu.SemaphoreType.DMA((3, max(n, 2))),
        ],
        compiler_params=pltpu.CompilerParams(vmem_limit_bytes=32 * MIB),
        cost_estimate=cost(2 * n),
        name="item_grads",
    )(at, terms, *messages, terms, items, *carried)


def local(queries, items, positive, tile_ids, counts):
    dp_at, shard_at = lax.axis_index("dp"), lax.axis_index("shard")
    n_dp, n_shard = lax.axis_size("dp"), lax.axis_size("shard")
    rows, width = queries.shape
    local_rows = items.shape[0]
    span_rows = 2 * (local_rows // n_dp)
    n_chips = n_dp // 2
    at = jnp.stack([shard_at, shard_at * local_rows, (dp_at // 2) * (span_rows // TILE), dp_at % 2]).astype(jnp.int32)

    message = pack(queries, positive, tile_ids, counts)
    group = plane(message, True)
    near = [swap(m, "dp", 2) for m in group]
    far, last = [], near[0]
    for k in range(2, n_chips):
        last = swap(after(message, last), "dp", 2 * k)
        far.append(last)
    groups = [group, near] + [plane(m, i % 2 == 0) for i, m in enumerate(far)]

    acc0, chosen0, stat0 = stats(group[:1], [], items, at)
    acc1, chosen1, stat1 = stats(group[1:3], [stat0], items, at)
    acc2, chosen2, stat = stats(group[3:], [stat1], items, at)
    all_stats = [stat] + [swap(stat, "shard", j) for j in range(1, n_shard)]
    loss, sent, shares = dq_shares(all_stats, [acc0, acc1, acc2], [chosen0, chosen1, chosen2])

    terms = [sent] + [swap(sent, "dp", 2 * k) for k in range(1, n_chips)]
    query_grad = shares[0] + sum(swap(shares[j], "shard", j) for j in range(1, n_shard))

    grads = None
    for k in range(n_chips):
        grads = item_grads(groups[k], terms[k], items, grads, span_rows, at, k == n_chips - 1)
    mine, other = grads
    item_grad = mine + swap(other, "dp", 1)
    return loss.reshape(rows), query_grad, item_grad


def solution(mesh):
    placed = (
        P(("dp", "shard"), None),
        P("shard", None),
        P(("dp", "shard")),
        P(("dp", "shard"), None, None),
        P(("dp", "shard"), None),
    )
    return jax.shard_map(
        local,
        mesh=mesh,
        in_specs=placed,
        out_specs=(P(("dp", "shard")), P(("dp", "shard"), None), P(("shard", "dp"), None)),
        check_vma=False,
    )
```

```python
import functools

import jax
import jax.numpy as jnp
from jax import lax
from jax.experimental import pallas as pl
from jax.experimental.pallas import tpu as pltpu
from jax.sharding import PartitionSpec as P

TILE = 512
KMAX = 3
EXTRA = 8
STEP = 4
STAT = 4
MIB = 1024 * 1024
VMEM_LIMIT = 12 * MIB

very_low = -1e30
high, highest = lax.Precision.HIGH, lax.Precision.HIGHEST

smem = pl.BlockSpec(memory_space=pltpu.SMEM)
vmem = pl.BlockSpec(memory_space=pltpu.VMEM)
anywhere = pl.BlockSpec(memory_space=pl.ANY)
hbm = pl.BlockSpec(memory_space=pltpu.HBM)


def dot(a, b, dims=((1,), (0,)), precision=high):
    return lax.dot_general(a, b, (dims, ((), ())), precision=precision, preferred_element_type=jnp.float32)


def cost(us):
    return pl.CostEstimate(flops=0, bytes_accessed=int(us * 3.0e6), transcendentals=0)


def pack_kernel(step, ids_ref, counts_ref, q_ref, pos_ref, out_ref, sem):
    rows, width = q_ref.shape
    get_q = pltpu.make_async_copy(q_ref, out_ref.at[:rows], sem)
    get_q.start()
    out_ref[rows : rows + EXTRA, :] = jnp.zeros((EXTRA, width), jnp.float32)
    row = pos_ref[...].astype(jnp.float32)
    col = jnp.broadcast_to(row, (8, rows)).T[:, 0:1]
    at_row = lax.broadcasted_iota(jnp.int32, (rows, rows), 1)
    at_col = lax.broadcasted_iota(jnp.int32, (rows, rows), 0)
    before = (row < col) | ((row == col) & (at_row < at_col))
    rank = jnp.sum(before.astype(jnp.float32), axis=1, keepdims=True)
    placed = rank == at_row.astype(jnp.float32)
    sorted_pos = jnp.sum(jnp.where(placed, col, 0.0), axis=0, keepdims=True)
    sorted_at = jnp.sum(jnp.where(placed, at_col.astype(jnp.float32), 0.0), axis=0, keepdims=True)
    starts = lax.broadcasted_iota(jnp.int32, (rows, width), 1).astype(jnp.float32) * step
    bounds = jnp.sum((col < starts).astype(jnp.float32), axis=0, keepdims=True)
    lane = lax.broadcasted_iota(jnp.int32, (1, width), 1)
    lists = jnp.zeros((1, width), jnp.int32)
    n = counts_ref.shape[1]
    for i in range(n * KMAX):
        lists = jnp.where(lane == i, ids_ref[0, i // KMAX, i % KMAX], lists)
    for i in range(n):
        lists = jnp.where(lane == n * KMAX + i, counts_ref[0, i], lists)
    per = rows // width
    out_ref[rows + 3 * per : rows + 3 * per + 1, :] = lists.astype(jnp.float32)
    out_ref[rows + 3 * per + 1 : rows + 3 * per + 2, :] = bounds
    for first, values in ((0, row), (per, sorted_pos), (2 * per, sorted_at)):
        for i in range(per):
            out_ref[rows + first + i : rows + first + i + 1, :] = values[:, i * width : (i + 1) * width]
    get_q.wait()


def pack(queries, positive, tile_ids, counts, step):
    rows, width = queries.shape
    return pl.pallas_call(
        functools.partial(pack_kernel, float(step)),
        out_shape=jax.ShapeDtypeStruct((rows + EXTRA, width), jnp.float32),
        in_specs=[smem, smem, anywhere, vmem],
        out_specs=vmem,
        scratch_shapes=[pltpu.SemaphoreType.DMA],
        compiler_params=pltpu.CompilerParams(vmem_limit_bytes=VMEM_LIMIT),
        cost_estimate=cost(2),
        name="pack",
    )(tile_ids, counts, queries, positive.reshape(1, rows))


class Lists:
    def __init__(self, ref, rows, shard_at, n_shard):
        self.ref, self.rows, self.shard_at, self.n_shard = ref, rows, shard_at, n_shard
        self.width = ref.shape[2]
        self.per = rows // self.width
        self.shift = self.width.bit_length() - 1

    def entry(self, b, first, i):
        return self.ref[b, first + (i >> self.shift), i & (self.width - 1)]

    def sorted_pos(self, b, i):
        return self.entry(b, self.per, i)

    def place(self, b, i):
        return self.entry(b, 2 * self.per, i)

    def tile(self, b, k):
        return self.ref[b, 3 * self.per, self.shard_at * KMAX + k]

    def count(self, b):
        return self.ref[b, 3 * self.per, self.n_shard * KMAX + self.shard_at]

    def bound(self, b, i):
        return self.ref[b, 3 * self.per + 1, i]


def swap(x, axis, bits):
    return lax.ppermute(x, axis, [(i, i ^ bits) for i in range(lax.axis_size(axis))])


def together(*xs):
    return lax.optimization_barrier(xs)


def stats_kernel(n, n_before, n_shard, at, *refs):
    msgs, refs = refs[:n], refs[n:]
    befores, refs = refs[:n_before], refs[n_before:]
    items_hbm, acc_ref, chosen_ref, stat_ref, q_ref, tiles, rowbuf, whole, lists_ref, sems, row_sems = refs
    rows = q_ref.shape[1] - EXTRA
    width = q_ref.shape[2]
    per = rows // width
    lists = Lists(lists_ref, rows, at[0], n_shard)
    base, local_rows = at[1], items_hbm.shape[0]
    get_lists = pltpu.make_async_copy(whole, lists_ref, sems.at[1, 0])

    def get_q(j):
        return pltpu.make_async_copy(msgs[j], q_ref.at[j], sems.at[0, j])

    def get_tile(b, k):
        start = pl.multiple_of(lists.tile(b, k) * TILE, TILE)
        return pltpu.make_async_copy(items_hbm.at[pl.ds(start, TILE)], tiles.at[b * KMAX + k], sems.at[2 + k, b])

    def get_row(b, i):
        return pltpu.make_async_copy(
            items_hbm.at[pl.ds(lists.sorted_pos(b, i) - base, 1)], rowbuf.at[b, pl.ds(lists.place(b, i), 1)], row_sems.at[b]
        )

    def row_loop(b):
        return pl.loop(lists.bound(b, at[0] * at[4]), lists.bound(b, (at[0] + 1) * at[4]))

    for j in range(n):
        get_q(j).start()
    rowbuf[...] = jnp.zeros(rowbuf.shape, jnp.float32)
    first = 0
    for before in befores:
        stat_ref[first : first + before.shape[0]] = before[...]
        first += before.shape[0]
    for j in range(n):
        get_q(j).wait()
    whole[...] = q_ref[:, rows:, :].astype(jnp.int32)
    get_lists.start()
    get_lists.wait()

    @pl.loop(0, n)
    def _(b):
        @pl.loop(0, lists.count(b))
        def _(k):
            get_tile(b, k).start()

    @pl.loop(0, n)
    def _(b):
        @row_loop(b)
        def _(i):
            get_row(b, i).start()

    @pl.loop(0, n)
    def _(b):
        q_t = q_ref[b, :rows, :].T
        acc_ref[b] = jnp.zeros(acc_ref.shape[1:], jnp.float32)

        def visit(k, carry):
            top, total = carry
            get_tile(b, k).wait()
            tile = tiles[b * KMAX + k]
            logits = dot(tile, q_t, precision=highest)
            new_top = jnp.maximum(top, jnp.max(logits, axis=0, keepdims=True))
            prob = jnp.exp(logits - new_top)
            scale = jnp.exp(top - new_top)
            total = total * scale + jnp.sum(prob, axis=0, keepdims=True)
            acc_ref[b] = acc_ref[b] * scale + dot(tile.T, prob)
            return new_top, total

        start = (jnp.full((1, rows), very_low, jnp.float32), jnp.zeros((1, rows), jnp.float32))
        top, total = lax.fori_loop(0, lists.count(b), visit, start)

        @row_loop(b)
        def _(i):
            get_row(b, i).wait()

        chosen = rowbuf[b].T
        chosen_ref[b] = chosen
        pos = jnp.concatenate([q_ref[b, rows + i : rows + i + 1, :] for i in range(per)], axis=1).astype(jnp.int32)
        offset = pos - base
        inside = (offset >= 0) & (offset < local_rows)
        plogit = jnp.sum(q_t * chosen, axis=0, keepdims=True)
        new_top = jnp.maximum(top, jnp.where(inside, plogit, very_low))
        total = total * jnp.exp(top - new_top) + jnp.where(inside, jnp.exp(plogit - new_top), 0.0)
        stat_ref[first + b, 0:1, :] = top
        stat_ref[first + b, 1:2, :] = new_top + jnp.log(total)
        stat_ref[first + b, 2:3, :] = jnp.where(inside, plogit, 0.0)
        stat_ref[first + b, 3:4, :] = jnp.where(inside, 1.0, 0.0)


def stats(messages, befores, items, at):
    n = len(messages)
    rows, width = messages[0].shape[0] - EXTRA, messages[0].shape[1]
    total = n + sum(b.shape[0] for b in befores)
    sums = jax.ShapeDtypeStruct((n, width, rows), jnp.float32)
    return pl.pallas_call(
        functools.partial(stats_kernel, n, len(befores), lax.axis_size("shard")),
        out_shape=(sums, sums, jax.ShapeDtypeStruct((total, STAT, rows), jnp.float32)),
        in_specs=[smem] + [anywhere] * n + [vmem] * len(befores) + [hbm],
        out_specs=(vmem, vmem, vmem),
        scratch_shapes=[
            pltpu.VMEM((n, rows + EXTRA, width), jnp.float32),
            pltpu.VMEM((n * KMAX, TILE, width), jnp.float32),
            pltpu.VMEM((n, rows, width), jnp.float32),
            pltpu.VMEM((n, EXTRA, width), jnp.int32),
            pltpu.SMEM((n, EXTRA, width), jnp.int32),
            pltpu.SemaphoreType.DMA((2 + KMAX, n)),
            pltpu.SemaphoreType.DMA((n,)),
        ],
        compiler_params=pltpu.CompilerParams(vmem_limit_bytes=VMEM_LIMIT + n * 3 * MIB),
        cost_estimate=cost(5 * n),
        name="stats",
    )(at, *messages, *befores, items)


def dq_kernel(n, counts, *refs):
    stat_refs, refs = refs[:n], refs[n:]
    acc_refs, refs = refs[: len(counts)], refs[len(counts) :]
    chosen_refs, refs = refs[: len(counts)], refs[len(counts) :]
    loss_ref, term_ref, share_refs = refs[0], refs[1], refs[2:]
    b = 0
    for acc_ref, chosen_ref, count in zip(acc_refs, chosen_refs, counts):
        for i in range(count):
            parts = [stat_refs[j][b ^ j, 1:2, :] for j in range(n)]
            top = functools.reduce(jnp.maximum, parts)
            lse = top + jnp.log(sum(jnp.exp(p - top) for p in parts))
            plogit = sum(stat_refs[j][b ^ j, 2:3, :] for j in range(n))
            weight = jnp.exp(plogit - lse) - 1.0
            term_ref[0, b : b + 1, :] = lse
            term_ref[1, b : b + 1, :] = weight
            if b == 0:
                loss_ref[...] = lse - plogit
            own = stat_refs[0]
            share = acc_ref[i] * jnp.exp(own[b, 0:1, :] - lse) + chosen_ref[i] * (weight * own[b, 3:4, :])
            share_refs[b][...] = share.T
            b += 1


def dq_shares(all_stats, accs, chosens):
    n, _, rows = all_stats[0].shape
    width = accs[0].shape[1]
    share = jax.ShapeDtypeStruct((rows, width), jnp.float32)
    loss, terms, *shares = pl.pallas_call(
        functools.partial(dq_kernel, n, [a.shape[0] for a in accs]),
        out_shape=(jax.ShapeDtypeStruct((1, rows), jnp.float32), jax.ShapeDtypeStruct((2, n, rows), jnp.float32), *[share] * n),
        compiler_params=pltpu.CompilerParams(vmem_limit_bytes=VMEM_LIMIT),
        cost_estimate=cost(3),
        name="dq",
    )(*all_stats, *accs, *chosens)
    return loss, terms, shares


def item_kernel(n, n_shard, n_waits, is_first, is_last, at, weight, *refs):
    msgs, refs = refs[:n], refs[n + n_waits :]
    lse_ref, items, refs = refs[0], refs[1], refs[2 if is_first else 3 :]
    acc, token, refs = refs[0], refs[1], refs[2:]
    if is_first:
        source, items, refs = items, refs[0], refs[1:]
    outs, refs = refs[: 2 * is_last], refs[2 * is_last :]
    q_ref, whole, lists_ref, sems = refs
    rows, width = q_ref.shape[1] - EXTRA, q_ref.shape[2]
    span_rows = acc.shape[0]
    tiles = span_rows // TILE
    base, first_tile, core = at[1] + at[2] * TILE, at[2], at[3]
    chip = at[0] * at[4] + at[5]
    lists = Lists(lists_ref, rows, at[0], n_shard)
    get_lists = pltpu.make_async_copy(whole, lists_ref, sems.at[1, 0])

    def get_q(j):
        return pltpu.make_async_copy(msgs[j], q_ref.at[j], sems.at[0, j])

    for j in range(n):
        get_q(j).start()
    if is_first:
        start = pl.multiple_of(first_tile * TILE, TILE)
        get_items = pltpu.make_async_copy(source.at[pl.ds(start, span_rows)], items, sems.at[2, 0])
        get_items.start()
        acc[...] = jnp.zeros(acc.shape, jnp.float32)
    token[...] = jnp.zeros(token.shape, jnp.float32)
    for j in range(n):
        get_q(j).wait()
    whole[...] = q_ref[:, rows:, :].astype(jnp.int32)
    get_lists.start()
    get_lists.wait()

    @pl.loop(0, n)
    def _(b):
        low, top = lists.bound(b, chip), lists.bound(b, chip + 1)

        @pl.loop(0, (top - low + STEP - 1) // STEP)
        def _(c):
            entries = [jnp.minimum(low + c * STEP + u, top - 1) for u in range(STEP)]
            rests = [jnp.where(low + c * STEP + u < top, 1.0, 0.0) for u in range(STEP)]
            heres = [lists.sorted_pos(b, i) - base for i in entries]
            places = [lists.place(b, i) for i in entries]
            olds = [acc[pl.ds(h, 1), :] for h in heres]
            terms = [q_ref[b, pl.ds(p, 1), :] * (weight[1, b, p] * r) for p, r in zip(places, rests)]
            for u in range(1, STEP):
                terms[u] = terms[u] + terms[u - 1] * jnp.where(heres[u] == heres[u - 1], 1.0, 0.0)
            for h, old, term in zip(heres, olds, terms):
                acc[pl.ds(h, 1), :] = old + term

    if is_first:
        get_items.wait()

    @pl.loop(0, n)
    def _(b):
        @pl.loop(0, lists.count(b))
        def _(k):
            tile = lists.tile(b, k) - first_tile

            @pl.when((tile >= 0) & (tile < tiles))
            def _():
                here = pl.ds(pl.multiple_of(tile * TILE, TILE), TILE)
                q = q_ref[b, :rows, :]
                logits = dot(items[here, :], q, ((1,), (1,)), highest)
                prob = jnp.exp(logits - lse_ref[0, pl.ds(b, 1), :])
                acc[here, :] += dot(prob, q)

    if is_last:
        own = span_rows // 2
        mine, other = outs
        put = [
            pltpu.make_async_copy(acc.at[pl.ds(pl.multiple_of((1 - core) * own, 8), own)], other, sems.at[2, 0]),
            pltpu.make_async_copy(acc.at[pl.ds(pl.multiple_of(core * own, 8), own)], mine, sems.at[2, 1]),
        ]
        for p in put:
            p.start()
        for p in put:
            p.wait()


def item_grads(messages, terms, items, acc, span_rows, at, is_last, waits=()):
    n = len(messages)
    rows, width = messages[0].shape[0] - EXTRA, messages[0].shape[1]
    is_first = acc is None
    half = jax.ShapeDtypeStruct((span_rows // 2, width), jnp.float32)
    chips = pltpu.VMEM((span_rows, width), jnp.float32)
    token = jax.ShapeDtypeStruct((1, 128), jnp.float32)
    more = [chips] if is_first else [half, half] if is_last else []
    carried = [] if is_first else [acc]
    return pl.pallas_call(
        functools.partial(item_kernel, n, lax.axis_size("shard"), len(waits), is_first, is_last),
        out_shape=(chips, token, *more),
        in_specs=[smem] * 2 + [anywhere] * (n + len(waits)) + [vmem, hbm if is_first else vmem] + [vmem] * len(carried),
        out_specs=(vmem, vmem, *[vmem if is_first else anywhere] * len(more)),
        scratch_shapes=[
            pltpu.VMEM((n, rows + EXTRA, width), jnp.float32),
            pltpu.VMEM((n, EXTRA, width), jnp.int32),
            pltpu.SMEM((n, EXTRA, width), jnp.int32),
            pltpu.SemaphoreType.DMA((3, max(n, 2))),
        ],
        input_output_aliases={} if is_first else {4 + n + len(waits): 0},
        compiler_params=pltpu.CompilerParams(vmem_limit_bytes=VMEM_LIMIT),
        cost_estimate=cost(2 * n),
        name="item_grads",
    )(at, terms, *messages, *waits, terms, items, *carried)


def local(queries, items, positive, tile_ids, counts):
    dp_at, shard_at = lax.axis_index("dp"), lax.axis_index("shard")
    n_dp, n_shard = lax.axis_size("dp"), lax.axis_size("shard")
    rows, width = queries.shape
    local_rows = items.shape[0]
    span_rows = 2 * (local_rows // n_dp)
    n_chips = n_dp // 2
    chip_at = dp_at // 2
    at = jnp.stack([shard_at, shard_at * local_rows, chip_at * (span_rows // TILE), dp_at % 2, n_chips, chip_at])
    at = at.astype(jnp.int32)

    def top(j):
        return 1 << (j.bit_length() - 1)

    items = pltpu.with_memory_space_constraint(items, pltpu.HBM)
    message = pack(queries, positive, tile_ids, counts, span_rows)
    own = [message] + [swap(message, "shard", j) for j in (1, 2)]
    straight = [message] + [swap(message, "dp", 2 * k) for k in range(1, n_chips)]
    acc0, chosen0, stat0 = stats([message], [], items, at)
    own[1], own[2], stat0 = together(own[1], own[2], stat0)
    for j in range(3, n_shard):
        own.append(swap(own[j ^ top(j)], "shard", top(j)))
    near = [straight[1], swap(own[1], "dp", 2)]
    acc1, chosen1, stat1 = stats(own[1:3], [stat0], items, at)
    straight[1], straight[2], stat1, *own[3:] = together(straight[1], straight[2], stat1, *own[3:])
    near[0] = straight[1]
    far = {2: [straight[2]] + [swap(straight[2], "shard", j) for j in (1, 2)]}
    acc2, chosen2, stat = stats(own[3:], [stat1], items, at)

    all_stats = [stat]
    bit = 1
    while bit < n_shard:
        got = swap(jnp.stack(all_stats) if bit > 1 else stat, "shard", bit)
        all_stats += [got[j] for j in range(bit)] if bit > 1 else [got]
        bit *= 2
    all_stats[0], near[1], far[2][1], far[2][2], *straight[3:] = together(
        all_stats[0], near[1], far[2][1], far[2][2], *straight[3:]
    )
    loss, sent, shares = dq_shares(all_stats, [acc0, acc1, acc2], [chosen0, chosen1, chosen2])
    for j in range(3, n_shard):
        far[2].append(swap(far[2][j ^ top(j)], "shard", top(j)))

    grads, token, chip_items = item_grads(own, sent, items, None, span_rows, at, False)
    terms = [sent]
    bit = 1
    while bit < n_chips:
        got = swap(jnp.stack(terms) + token[0, 0] if bit > 1 else sent, "dp", 2 * bit)
        terms += [got[j] for j in range(bit)] if bit > 1 else [got]
        bit *= 2
    for k in range(3, n_chips):
        far[k] = [straight[k]] + [swap(straight[k], "shard", j) for j in (1, 2)]
    rest = jnp.concatenate(own[2:]) + jnp.minimum(jnp.abs(terms[n_chips - 1][0, 0, 0]), 0.0)
    rest = swap(rest, "dp", 2)
    size = rows + EXTRA
    near += [rest[i * size : (i + 1) * size] for i in range(n_shard - 2)]
    grads = item_grads(far[2], terms[2], chip_items, grads, span_rows, at, False)[0]

    for k in range(3, n_chips):
        for j in range(3, n_shard):
            far[k].append(swap(far[k][j ^ top(j)], "shard", top(j)))
    sums = dict(enumerate(shares))
    bit = 1
    while bit < n_shard:
        sums = {j: sums[j] + swap(sums[j ^ bit], "shard", bit) for j in sorted(sums, reverse=True) if not j & bit}
        bit *= 2
    query_grad = sums[0]
    grads = item_grads(near, terms[1], chip_items, grads, span_rows, at, False)[0]
    for k in range(3, n_chips):
        is_last = k == n_chips - 1
        out = item_grads(far[k], terms[k], chip_items, grads, span_rows, at, is_last, [query_grad] if is_last else [])
        grads = out[0]
    mine, other = out[2:]
    item_grad = mine + swap(other, "dp", 1)
    return loss.reshape(rows), query_grad, item_grad


def solution(mesh):
    placed = (
        P(("dp", "shard"), None),
        P("shard", None),
        P(("dp", "shard")),
        P(("dp", "shard"), None, None),
        P(("dp", "shard"), None),
    )
    return jax.shard_map(
        local,
        mesh=mesh,
        in_specs=placed,
        out_specs=(P(("dp", "shard")), P(("dp", "shard"), None), P(("shard", "dp"), None)),
        check_vma=False,
    )
```

```python
import functools

import jax
import jax.numpy as jnp
from jax import lax
from jax.experimental import pallas as pl
from jax.experimental.pallas import tpu as pltpu
from jax.sharding import PartitionSpec as P

TILE = 512
KMAX = 3
EXTRA = 8
LOADS = 8
GATHER = 8
STEP = 4
STAT = 4
MIB = 1024 * 1024
VMEM_LIMIT = 12 * MIB

very_low = -1e30
high, highest = lax.Precision.HIGH, lax.Precision.HIGHEST

smem = pl.BlockSpec(memory_space=pltpu.SMEM)
vmem = pl.BlockSpec(memory_space=pltpu.VMEM)
anywhere = pl.BlockSpec(memory_space=pl.ANY)
hbm = pl.BlockSpec(memory_space=pltpu.HBM)


def dot(a, b, dims=((1,), (0,)), precision=high):
    return lax.dot_general(a, b, (dims, ((), ())), precision=precision, preferred_element_type=jnp.float32)


def halves(x):
    upper = x.astype(jnp.bfloat16)
    return upper, (x - upper.astype(jnp.float32)).astype(jnp.bfloat16)


def dot3(a, b, dims=((1,), (0,))):
    def one(i, j):
        return lax.dot_general(a[i], b[j], (dims, ((), ())), preferred_element_type=jnp.float32)

    return (one(0, 1) + one(1, 0)) + one(0, 0)


def cost(us):
    return pl.CostEstimate(flops=0, bytes_accessed=int(us * 3.0e6), transcendentals=0)


def pack_kernel(step, ids_ref, counts_ref, q_ref, pos_ref, out_ref, sem):
    rows, width = q_ref.shape
    get_q = pltpu.make_async_copy(q_ref, out_ref.at[:rows], sem)
    get_q.start()
    out_ref[rows : rows + EXTRA, :] = jnp.zeros((EXTRA, width), jnp.float32)
    row = pos_ref[...].astype(jnp.float32)
    col = jnp.broadcast_to(row, (8, rows)).T[:, 0:1]
    at_row = lax.broadcasted_iota(jnp.int32, (rows, rows), 1)
    at_col = lax.broadcasted_iota(jnp.int32, (rows, rows), 0)
    before = (row < col) | ((row == col) & (at_row < at_col))
    rank = jnp.sum(before.astype(jnp.float32), axis=1, keepdims=True)
    placed = rank == at_row.astype(jnp.float32)
    sorted_pos = jnp.sum(jnp.where(placed, col, 0.0), axis=0, keepdims=True)
    sorted_at = jnp.sum(jnp.where(placed, at_col.astype(jnp.float32), 0.0), axis=0, keepdims=True)
    starts = lax.broadcasted_iota(jnp.int32, (rows, width), 1).astype(jnp.float32) * step
    bounds = jnp.sum((col < starts).astype(jnp.float32), axis=0, keepdims=True)
    lane = lax.broadcasted_iota(jnp.int32, (1, width), 1)
    lists = jnp.zeros((1, width), jnp.int32)
    n = counts_ref.shape[1]
    for i in range(n * KMAX):
        lists = jnp.where(lane == i, ids_ref[0, i // KMAX, i % KMAX], lists)
    for i in range(n):
        lists = jnp.where(lane == n * KMAX + i, counts_ref[0, i], lists)
    per = rows // width
    out_ref[rows + 3 * per : rows + 3 * per + 1, :] = lists.astype(jnp.float32)
    out_ref[rows + 3 * per + 1 : rows + 3 * per + 2, :] = bounds
    for first, values in ((0, row), (per, sorted_pos), (2 * per, sorted_at)):
        for i in range(per):
            out_ref[rows + first + i : rows + first + i + 1, :] = values[:, i * width : (i + 1) * width]
    get_q.wait()


def pack(queries, positive, tile_ids, counts, step):
    rows, width = queries.shape
    return pl.pallas_call(
        functools.partial(pack_kernel, float(step)),
        out_shape=jax.ShapeDtypeStruct((rows + EXTRA, width), jnp.float32),
        in_specs=[smem, smem, anywhere, vmem],
        out_specs=vmem,
        scratch_shapes=[pltpu.SemaphoreType.DMA],
        compiler_params=pltpu.CompilerParams(vmem_limit_bytes=VMEM_LIMIT),
        cost_estimate=cost(2),
        name="pack",
    )(tile_ids, counts, queries, positive.reshape(1, rows))


class Lists:
    def __init__(self, ref, rows, shard_at, n_shard):
        self.ref, self.rows, self.shard_at, self.n_shard = ref, rows, shard_at, n_shard
        self.width = ref.shape[2]
        self.per = rows // self.width
        self.shift = self.width.bit_length() - 1

    def entry(self, b, first, i):
        return self.ref[b, first + (i >> self.shift), i & (self.width - 1)]

    def sorted_pos(self, b, i):
        return self.entry(b, self.per, i)

    def place(self, b, i):
        return self.entry(b, 2 * self.per, i)

    def tile(self, b, k):
        return self.ref[b, 3 * self.per, self.shard_at * KMAX + k]

    def count(self, b):
        return self.ref[b, 3 * self.per, self.n_shard * KMAX + self.shard_at]

    def bound(self, b, i):
        return self.ref[b, 3 * self.per + 1, i]


def swap(x, axis, bits):
    return lax.ppermute(x, axis, [(i, i ^ bits) for i in range(lax.axis_size(axis))])


def none(*xs):
    return sum(jnp.minimum(jnp.abs(x[(0,) * x.ndim]), 0.0) for x in xs)


def together(*xs):
    return lax.optimization_barrier(xs)


def stats_kernel(n, n_before, n_shard, loads, at, *refs):
    msgs, refs = refs[:n], refs[n:]
    befores, refs = refs[:n_before], refs[n_before:]
    source, acc_ref, chosen_ref, stat_ref, refs = refs[0], refs[1], refs[2], refs[3], refs[4:]
    items = source
    if loads:
        items, refs = refs[0], refs[1:]
    q_ref, rowbuf, whole, lists_ref, sems, load_sems = refs
    rows = q_ref.shape[1] - EXTRA
    width = q_ref.shape[2]
    per = rows // width
    lists = Lists(lists_ref, rows, at[0], n_shard)
    base, local_rows = at[1], items.shape[0]
    chunk = local_rows // LOADS
    get_lists = pltpu.make_async_copy(whole, lists_ref, sems.at[1, 0])

    def get_q(j):
        return pltpu.make_async_copy(msgs[j], q_ref.at[j], sems.at[0, j])

    def get_items(i):
        part = pl.ds(i * chunk, chunk)
        return pltpu.make_async_copy(source.at[part], items.at[part], load_sems.at[i])

    for j in range(n):
        get_q(j).start()
    if loads:
        for i in range(LOADS):
            get_items(i).start()
    first = 0
    for before in befores:
        stat_ref[first : first + before.shape[0]] = before[...]
        first += before.shape[0]
    for j in range(n):
        get_q(j).wait()
    whole[...] = q_ref[:, rows:, :].astype(jnp.int32)
    get_lists.start()
    get_lists.wait()
    if loads:
        for i in range(LOADS):
            get_items(i).wait()

    @pl.loop(0, n)
    def _(b):
        q_t = q_ref[b, :rows, :].T
        q_halves = halves(q_t)
        acc_ref[b] = jnp.zeros(acc_ref.shape[1:], jnp.float32)
        rowbuf[...] = jnp.zeros(rowbuf.shape, jnp.float32)
        low, high_end = lists.bound(b, at[0] * at[4]), lists.bound(b, (at[0] + 1) * at[4])

        @pl.loop(0, (high_end - low + GATHER - 1) // GATHER)
        def _(c):
            entries = [jnp.minimum(low + c * GATHER + u, high_end - 1) for u in range(GATHER)]
            got = [items[pl.ds(lists.sorted_pos(b, i) - base, 1), :] for i in entries]
            for i, row in zip(entries, got):
                rowbuf[pl.ds(lists.place(b, i), 1), :] = row

        def visit(k, carry):
            top, total = carry
            tile = items[pl.ds(pl.multiple_of(lists.tile(b, k) * TILE, TILE), TILE), :]
            logits = dot3(halves(tile), q_halves)
            new_top = jnp.maximum(top, jnp.max(logits, axis=0, keepdims=True))
            prob = jnp.exp(logits - new_top)
            scale = jnp.exp(top - new_top)
            total = total * scale + jnp.sum(prob, axis=0, keepdims=True)
            acc_ref[b] = acc_ref[b] * scale + dot(tile.T, prob)
            return new_top, total

        start = (jnp.full((1, rows), very_low, jnp.float32), jnp.zeros((1, rows), jnp.float32))
        top, total = lax.fori_loop(0, lists.count(b), visit, start)

        chosen = rowbuf[...].T
        chosen_ref[b] = chosen
        pos = jnp.concatenate([q_ref[b, rows + i : rows + i + 1, :] for i in range(per)], axis=1).astype(jnp.int32)
        offset = pos - base
        inside = (offset >= 0) & (offset < local_rows)
        plogit = jnp.sum(q_t * chosen, axis=0, keepdims=True)
        new_top = jnp.maximum(top, jnp.where(inside, plogit, very_low))
        total = total * jnp.exp(top - new_top) + jnp.where(inside, jnp.exp(plogit - new_top), 0.0)
        stat_ref[first + b, 0:1, :] = top
        stat_ref[first + b, 1:2, :] = new_top + jnp.log(total)
        stat_ref[first + b, 2:3, :] = jnp.where(inside, plogit, 0.0)
        stat_ref[first + b, 3:4, :] = jnp.where(inside, 1.0, 0.0)


def stats(messages, befores, items, at, loads):
    n = len(messages)
    rows, width = messages[0].shape[0] - EXTRA, messages[0].shape[1]
    total = n + sum(b.shape[0] for b in befores)
    sums = jax.ShapeDtypeStruct((n, width, rows), jnp.float32)
    held = [pltpu.VMEM(items.shape, jnp.float32)] if loads else []
    return pl.pallas_call(
        functools.partial(stats_kernel, n, len(befores), lax.axis_size("shard"), loads),
        out_shape=(sums, sums, jax.ShapeDtypeStruct((total, STAT, rows), jnp.float32), *held),
        in_specs=[smem] + [anywhere] * n + [vmem] * len(befores) + [hbm if loads else vmem],
        out_specs=(vmem, vmem, vmem, *[vmem] * len(held)),
        scratch_shapes=[
            pltpu.VMEM((n, rows + EXTRA, width), jnp.float32),
            pltpu.VMEM((rows, width), jnp.float32),
            pltpu.VMEM((n, EXTRA, width), jnp.int32),
            pltpu.SMEM((n, EXTRA, width), jnp.int32),
            pltpu.SemaphoreType.DMA((2, n)),
            pltpu.SemaphoreType.DMA((LOADS,)),
        ],
        compiler_params=pltpu.CompilerParams(vmem_limit_bytes=VMEM_LIMIT),
        cost_estimate=cost(5 * n),
        name="stats",
    )(at, *messages, *befores, items)


def dq_kernel(n, counts, *refs):
    stat_refs, refs = refs[:n], refs[n:]
    acc_refs, refs = refs[: len(counts)], refs[len(counts) :]
    chosen_refs, refs = refs[: len(counts)], refs[len(counts) :]
    loss_ref, term_ref, share_refs = refs[0], refs[1], refs[2:]
    b = 0
    for acc_ref, chosen_ref, count in zip(acc_refs, chosen_refs, counts):
        for i in range(count):
            parts = [stat_refs[j][b ^ j, 1:2, :] for j in range(n)]
            top = functools.reduce(jnp.maximum, parts)
            lse = top + jnp.log(sum(jnp.exp(p - top) for p in parts))
            plogit = sum(stat_refs[j][b ^ j, 2:3, :] for j in range(n))
            weight = jnp.exp(plogit - lse) - 1.0
            term_ref[0, b : b + 1, :] = lse
            term_ref[1, b : b + 1, :] = weight
            if b == 0:
                loss_ref[...] = lse - plogit
            own = stat_refs[0]
            share = acc_ref[i] * jnp.exp(own[b, 0:1, :] - lse) + chosen_ref[i] * (weight * own[b, 3:4, :])
            share_refs[b][...] = share.T
            b += 1


def dq_shares(all_stats, accs, chosens):
    n, _, rows = all_stats[0].shape
    width = accs[0].shape[1]
    share = jax.ShapeDtypeStruct((rows, width), jnp.float32)
    loss, terms, *shares = pl.pallas_call(
        functools.partial(dq_kernel, n, [a.shape[0] for a in accs]),
        out_shape=(jax.ShapeDtypeStruct((1, rows), jnp.float32), jax.ShapeDtypeStruct((2, n, rows), jnp.float32), *[share] * n),
        compiler_params=pltpu.CompilerParams(vmem_limit_bytes=VMEM_LIMIT),
        cost_estimate=cost(3),
        name="dq",
    )(*all_stats, *accs, *chosens)
    return loss, terms, shares


def item_kernel(n, n_shard, n_waits, is_first, is_last, at, weight, *refs):
    msgs, refs = refs[:n], refs[n + n_waits :]
    lse_ref, items, refs = refs[0], refs[1], refs[2 if is_first else 3 :]
    acc, token, refs = refs[0], refs[1], refs[2:]
    if is_first:
        source, items, refs = items, refs[0], refs[1:]
    outs, refs = refs[: 2 * is_last], refs[2 * is_last :]
    q_ref, whole, lists_ref, sems = refs
    rows, width = q_ref.shape[1] - EXTRA, q_ref.shape[2]
    span_rows = acc.shape[0]
    tiles = span_rows // TILE
    base, first_tile, core = at[1] + at[2] * TILE, at[2], at[3]
    chip = at[0] * at[4] + at[5]
    lists = Lists(lists_ref, rows, at[0], n_shard)
    get_lists = pltpu.make_async_copy(whole, lists_ref, sems.at[1, 0])

    def get_q(j):
        return pltpu.make_async_copy(msgs[j], q_ref.at[j], sems.at[0, j])

    for j in range(n):
        get_q(j).start()
    if is_first:
        start = pl.multiple_of(first_tile * TILE, TILE)
        get_items = pltpu.make_async_copy(source.at[pl.ds(start, span_rows)], items, sems.at[2, 0])
        get_items.start()
        acc[...] = jnp.zeros(acc.shape, jnp.float32)
    token[...] = jnp.zeros(token.shape, jnp.float32)
    for j in range(n):
        get_q(j).wait()
    whole[...] = q_ref[:, rows:, :].astype(jnp.int32)
    get_lists.start()
    get_lists.wait()

    @pl.loop(0, n)
    def _(b):
        low, top = lists.bound(b, chip), lists.bound(b, chip + 1)

        @pl.loop(0, (top - low + STEP - 1) // STEP)
        def _(c):
            entries = [jnp.minimum(low + c * STEP + u, top - 1) for u in range(STEP)]
            rests = [jnp.where(low + c * STEP + u < top, 1.0, 0.0) for u in range(STEP)]
            heres = [lists.sorted_pos(b, i) - base for i in entries]
            places = [lists.place(b, i) for i in entries]
            olds = [acc[pl.ds(h, 1), :] for h in heres]
            terms = [q_ref[b, pl.ds(p, 1), :] * (weight[1, b, p] * r) for p, r in zip(places, rests)]
            for u in range(1, STEP):
                terms[u] = terms[u] + terms[u - 1] * jnp.where(heres[u] == heres[u - 1], 1.0, 0.0)
            for h, old, term in zip(heres, olds, terms):
                acc[pl.ds(h, 1), :] = old + term

    if is_first:
        get_items.wait()

    @pl.loop(0, n)
    def _(b):
        @pl.loop(0, lists.count(b))
        def _(k):
            tile = lists.tile(b, k) - first_tile

            @pl.when((tile >= 0) & (tile < tiles))
            def _():
                here = pl.ds(pl.multiple_of(tile * TILE, TILE), TILE)
                q = q_ref[b, :rows, :]
                logits = dot3(halves(items[here, :]), halves(q), ((1,), (1,)))
                prob = jnp.exp(logits - lse_ref[0, pl.ds(b, 1), :])
                acc[here, :] += dot(prob, q)

    if is_last:
        own = span_rows // 2
        mine, other = outs
        put = [
            pltpu.make_async_copy(acc.at[pl.ds(pl.multiple_of((1 - core) * own, 8), own)], other, sems.at[2, 0]),
            pltpu.make_async_copy(acc.at[pl.ds(pl.multiple_of(core * own, 8), own)], mine, sems.at[2, 1]),
        ]
        for p in put:
            p.start()
        for p in put:
            p.wait()


def item_grads(messages, terms, items, acc, span_rows, at, is_last, waits=()):
    n = len(messages)
    rows, width = messages[0].shape[0] - EXTRA, messages[0].shape[1]
    is_first = acc is None
    half = jax.ShapeDtypeStruct((span_rows // 2, width), jnp.float32)
    chips = pltpu.VMEM((span_rows, width), jnp.float32)
    token = jax.ShapeDtypeStruct((1, 128), jnp.float32)
    more = [chips] if is_first else [half, half] if is_last else []
    carried = [] if is_first else [acc]
    return pl.pallas_call(
        functools.partial(item_kernel, n, lax.axis_size("shard"), len(waits), is_first, is_last),
        out_shape=(chips, token, *more),
        in_specs=[smem] * 2 + [anywhere] * (n + len(waits)) + [vmem, hbm if is_first else vmem] + [vmem] * len(carried),
        out_specs=(vmem, vmem, *[vmem if is_first else anywhere] * len(more)),
        scratch_shapes=[
            pltpu.VMEM((n, rows + EXTRA, width), jnp.float32),
            pltpu.VMEM((n, EXTRA, width), jnp.int32),
            pltpu.SMEM((n, EXTRA, width), jnp.int32),
            pltpu.SemaphoreType.DMA((3, max(n, 2))),
        ],
        input_output_aliases={} if is_first else {4 + n + len(waits): 0},
        compiler_params=pltpu.CompilerParams(vmem_limit_bytes=VMEM_LIMIT),
        cost_estimate=cost(2 * n),
        name="item_grads",
    )(at, terms, *messages, *waits, terms, items, *carried)


def local(queries, items, positive, tile_ids, counts):
    dp_at, shard_at = lax.axis_index("dp"), lax.axis_index("shard")
    n_dp, n_shard = lax.axis_size("dp"), lax.axis_size("shard")
    rows, width = queries.shape
    local_rows = items.shape[0]
    span_rows = 2 * (local_rows // n_dp)
    n_chips = n_dp // 2
    chip_at = dp_at // 2
    at = jnp.stack([shard_at, shard_at * local_rows, chip_at * (span_rows // TILE), dp_at % 2, n_chips, chip_at])
    at = at.astype(jnp.int32)

    def top(j):
        return 1 << (j.bit_length() - 1)

    items = pltpu.with_memory_space_constraint(items, pltpu.HBM)
    message = pack(queries, positive, tile_ids, counts, span_rows)
    own = [message] + [swap(message, "shard", j) for j in (1, 2)]
    straight = [message, None, swap(message, "dp", 4)]
    acc0, chosen0, stat0, held = stats([message], [], items, at, True)

    message, own[1], own[2], stat0 = together(message, own[1], own[2], stat0)
    straight[1] = swap(message, "dp", 2)
    for j in range(3, n_shard):
        own.append(swap(own[j ^ top(j)], "shard", top(j)))
    acc1, chosen1, stat1 = stats(own[1:3], [stat0], held, at, False)

    message, straight[2], stat1, *own[3:] = together(message, straight[2], stat1, *own[3:])
    straight += [swap(message, "dp", 2 * k) for k in range(3, n_chips)]
    far = {2: [straight[2]] + [swap(straight[2], "shard", j) for j in (1, 2)]}
    acc2, chosen2, stat = stats(own[3:], [stat1], held, at, False)

    all_stats = [stat]
    bit = 1
    while bit < n_shard:
        got = swap(jnp.stack(all_stats) if bit > 1 else stat, "shard", bit)
        all_stats += [got[j] for j in range(bit)] if bit > 1 else [got]
        bit *= 2
    all_stats[-1], far[2][1], far[2][2], straight[1], *straight[3:] = together(
        all_stats[-1], far[2][1], far[2][2], straight[1], *straight[3:]
    )
    loss, sent, shares = dq_shares(all_stats, [acc0, acc1, acc2], [chosen0, chosen1, chosen2])

    for k in range(3, n_chips):
        far[k] = [straight[k]] + [swap(straight[k], "shard", j) for j in (1, 2)]
    for j in range(3, n_shard):
        far[2].append(swap(far[2][j & (j - 1)], "shard", j & -j))
    near = [straight[1], swap(own[1], "dp", 2)]
    grads, token, chip_items = item_grads(own, sent, items, None, span_rows, at, False)
    first = [far[2][3], *[far[k][2] for k in range(3, n_chips)]]
    terms = [sent]
    bit = 1
    while bit < n_chips:
        got = swap(jnp.stack(terms) + none(token, *first) if bit > 1 else sent, "dp", 2 * bit)
        terms += [got[j] for j in range(bit)] if bit > 1 else [got]
        bit *= 2

    for k in range(3, n_chips):
        for j in range(3, n_shard):
            far[k].append(swap(far[k][j & (j - 1)], "shard", j & -j))
    sums = dict(enumerate(shares))
    bit = n_shard // 2
    sums = {j: sums[j] + swap(sums[j ^ bit], "shard", bit) for j in sorted(sums, reverse=True) if not j & bit}
    near += [swap(own[j] + none(terms[n_chips - 1]), "dp", 2) for j in range(2, n_shard)]
    grads, token = item_grads(far[2], terms[2], chip_items, grads, span_rows, at, False, [near[1]])[:2]

    early = far[n_chips - 1][3]
    while bit > 1:
        bit //= 2
        sums = {j: x + none(early) if j & bit else x for j, x in sums.items()}
        sums = {j: sums[j] + swap(sums[j ^ bit], "shard", bit) for j in sorted(sums, reverse=True) if not j & bit}
    query_grad = sums[0]
    for k in range(3, n_chips):
        grads = item_grads(far[k], terms[k], chip_items, grads, span_rows, at, False, [near[2]])[0]
    mine, other = item_grads(near, terms[1], chip_items, grads, span_rows, at, True, [query_grad])[2:]
    item_grad = mine + swap(other, "dp", 1)
    return loss.reshape(rows), query_grad, item_grad


def solution(mesh):
    placed = (
        P(("dp", "shard"), None),
        P("shard", None),
        P(("dp", "shard")),
        P(("dp", "shard"), None, None),
        P(("dp", "shard"), None),
    )
    return jax.shard_map(
        local,
        mesh=mesh,
        in_specs=placed,
        out_specs=(P(("dp", "shard")), P(("dp", "shard"), None), P(("shard", "dp"), None)),
        check_vma=False,
    )
```

```python
import functools

import jax
import jax.numpy as jnp
from jax import lax
from jax.experimental import pallas as pl
from jax.experimental.pallas import tpu as pltpu
from jax.sharding import PartitionSpec as P

TILE = 512
KMAX = 3
EXTRA = 8
LOADS = 8
GATHER = 8
STEP = 4
STAT = 4
MIB = 1024 * 1024
VMEM_LIMIT = 10 * MIB

very_low = -1e30
high, highest = lax.Precision.HIGH, lax.Precision.HIGHEST

smem = pl.BlockSpec(memory_space=pltpu.SMEM)
vmem = pl.BlockSpec(memory_space=pltpu.VMEM)
anywhere = pl.BlockSpec(memory_space=pl.ANY)
hbm = pl.BlockSpec(memory_space=pltpu.HBM)


def dot(a, b, dims=((1,), (0,)), precision=high):
    return lax.dot_general(a, b, (dims, ((), ())), precision=precision, preferred_element_type=jnp.float32)


def halves(x):
    upper = x.astype(jnp.bfloat16)
    return upper, (x - upper.astype(jnp.float32)).astype(jnp.bfloat16)


def dot3(a, b, dims=((1,), (0,))):
    def one(i, j):
        return lax.dot_general(a[i], b[j], (dims, ((), ())), preferred_element_type=jnp.float32)

    return (one(0, 1) + one(1, 0)) + one(0, 0)


def cost(us):
    return pl.CostEstimate(flops=0, bytes_accessed=int(us * 3.0e6), transcendentals=0)


def pack_kernel(step, ids_ref, counts_ref, q_ref, pos_ref, out_ref, sem):
    rows, width = q_ref.shape
    get_q = pltpu.make_async_copy(q_ref, out_ref.at[:rows], sem)
    get_q.start()
    out_ref[rows : rows + EXTRA, :] = jnp.zeros((EXTRA, width), jnp.float32)
    row = pos_ref[...].astype(jnp.float32)
    col = jnp.broadcast_to(row, (8, rows)).T[:, 0:1]
    at_row = lax.broadcasted_iota(jnp.int32, (rows, rows), 1)
    at_col = lax.broadcasted_iota(jnp.int32, (rows, rows), 0)
    before = (row < col) | ((row == col) & (at_row < at_col))
    rank = jnp.sum(before.astype(jnp.float32), axis=1, keepdims=True)
    placed = rank == at_row.astype(jnp.float32)
    sorted_pos = jnp.sum(jnp.where(placed, col, 0.0), axis=0, keepdims=True)
    sorted_at = jnp.sum(jnp.where(placed, at_col.astype(jnp.float32), 0.0), axis=0, keepdims=True)
    starts = lax.broadcasted_iota(jnp.int32, (rows, width), 1).astype(jnp.float32) * step
    bounds = jnp.sum((col < starts).astype(jnp.float32), axis=0, keepdims=True)
    lane = lax.broadcasted_iota(jnp.int32, (1, width), 1)
    lists = jnp.zeros((1, width), jnp.int32)
    n = counts_ref.shape[1]
    for i in range(n * KMAX):
        lists = jnp.where(lane == i, ids_ref[0, i // KMAX, i % KMAX], lists)
    for i in range(n):
        lists = jnp.where(lane == n * KMAX + i, counts_ref[0, i], lists)
    per = rows // width
    out_ref[rows + 3 * per : rows + 3 * per + 1, :] = lists.astype(jnp.float32)
    out_ref[rows + 3 * per + 1 : rows + 3 * per + 2, :] = bounds
    for first, values in ((0, row), (per, sorted_pos), (2 * per, sorted_at)):
        for i in range(per):
            out_ref[rows + first + i : rows + first + i + 1, :] = values[:, i * width : (i + 1) * width]
    get_q.wait()


def pack(queries, positive, tile_ids, counts, step):
    rows, width = queries.shape
    return pl.pallas_call(
        functools.partial(pack_kernel, float(step)),
        out_shape=jax.ShapeDtypeStruct((rows + EXTRA, width), jnp.float32),
        in_specs=[smem, smem, hbm, vmem],
        out_specs=vmem,
        scratch_shapes=[pltpu.SemaphoreType.DMA],
        compiler_params=pltpu.CompilerParams(vmem_limit_bytes=VMEM_LIMIT),
        cost_estimate=cost(2),
        name="pack",
    )(tile_ids, counts, queries, positive.reshape(1, rows))


class Lists:
    def __init__(self, ref, rows, shard_at, n_shard):
        self.ref, self.rows, self.shard_at, self.n_shard = ref, rows, shard_at, n_shard
        self.width = ref.shape[2]
        self.per = rows // self.width
        self.shift = self.width.bit_length() - 1

    def entry(self, b, first, i):
        return self.ref[b, first + (i >> self.shift), i & (self.width - 1)]

    def sorted_pos(self, b, i):
        return self.entry(b, self.per, i)

    def place(self, b, i):
        return self.entry(b, 2 * self.per, i)

    def tile(self, b, k):
        return self.ref[b, 3 * self.per, self.shard_at * KMAX + k]

    def count(self, b):
        return self.ref[b, 3 * self.per, self.n_shard * KMAX + self.shard_at]

    def bound(self, b, i):
        return self.ref[b, 3 * self.per + 1, i]


def swap(x, axis, bits):
    return lax.ppermute(x, axis, [(i, i ^ bits) for i in range(lax.axis_size(axis))])


def none(*xs):
    return sum(jnp.minimum(jnp.abs(x[(0,) * x.ndim]), 0.0) for x in xs)


def together(*xs):
    return lax.optimization_barrier(xs)


def stats_kernel(n, n_before, n_shard, loads, at, *refs):
    msgs, refs = refs[:n], refs[n:]
    befores, refs = refs[:n_before], refs[n_before:]
    source, acc_ref, chosen_ref, stat_ref, refs = refs[0], refs[1], refs[2], refs[3], refs[4:]
    items = source
    if loads:
        items, refs = refs[0], refs[1:]
    if loads:
        tiles, tile_sems, refs = refs[0], refs[1], refs[2:]
    q_ref, rowbuf, whole, lists_ref, sems, load_sems = refs
    rows = q_ref.shape[1] - EXTRA
    width = q_ref.shape[2]
    per = rows // width
    lists = Lists(lists_ref, rows, at[0], n_shard)
    base, local_rows = at[1], items.shape[0]
    chunk = local_rows // LOADS
    get_lists = pltpu.make_async_copy(whole, lists_ref, sems.at[1, 0])

    def get_q(j):
        return pltpu.make_async_copy(msgs[j], q_ref.at[j], sems.at[0, j])

    def get_items(i):
        part = pl.ds(i * chunk, chunk)
        return pltpu.make_async_copy(source.at[part], items.at[part], load_sems.at[i])

    def get_tile(k):
        start = pl.multiple_of(lists.tile(0, k) * TILE, TILE)
        return pltpu.make_async_copy(source.at[pl.ds(start, TILE)], tiles.at[k], tile_sems.at[k])

    for j in range(n):
        get_q(j).start()
    first = 0
    for before in befores:
        stat_ref[first : first + before.shape[0]] = before[...]
        first += before.shape[0]
    for j in range(n):
        get_q(j).wait()
    whole[...] = q_ref[:, rows:, :].astype(jnp.int32)
    get_lists.start()
    get_lists.wait()
    if loads:

        @pl.loop(0, lists.count(0))
        def _(k):
            get_tile(k).start()

        for i in range(LOADS):
            get_items(i).start()

    @pl.loop(0, n)
    def _(b):
        q_t = q_ref[b, :rows, :].T
        q_halves = halves(q_t)
        acc_ref[b] = jnp.zeros(acc_ref.shape[1:], jnp.float32)

        def visit(k, carry):
            top, total = carry
            if loads:
                get_tile(k).wait()
                tile = tiles[k]
            else:
                tile = items[pl.ds(pl.multiple_of(lists.tile(b, k) * TILE, TILE), TILE), :]
            logits = dot3(halves(tile), q_halves)
            new_top = jnp.maximum(top, jnp.max(logits, axis=0, keepdims=True))
            prob = jnp.exp(logits - new_top)
            scale = jnp.exp(top - new_top)
            total = total * scale + jnp.sum(prob, axis=0, keepdims=True)
            acc_ref[b] = acc_ref[b] * scale + dot(tile.T, prob)
            return new_top, total

        start = (jnp.full((1, rows), very_low, jnp.float32), jnp.zeros((1, rows), jnp.float32))
        top, total = lax.fori_loop(0, lists.count(b), visit, start)

        if loads:
            for i in range(LOADS):
                get_items(i).wait()
        rowbuf[...] = jnp.zeros(rowbuf.shape, jnp.float32)
        low, high_end = lists.bound(b, at[0] * at[4]), lists.bound(b, (at[0] + 1) * at[4])

        @pl.loop(0, (high_end - low + GATHER - 1) // GATHER)
        def _(c):
            entries = [jnp.minimum(low + c * GATHER + u, high_end - 1) for u in range(GATHER)]
            got = [items[pl.ds(lists.sorted_pos(b, i) - base, 1), :] for i in entries]
            for i, row in zip(entries, got):
                rowbuf[pl.ds(lists.place(b, i), 1), :] = row

        chosen = rowbuf[...].T
        chosen_ref[b] = chosen
        pos = jnp.concatenate([q_ref[b, rows + i : rows + i + 1, :] for i in range(per)], axis=1).astype(jnp.int32)
        offset = pos - base
        inside = (offset >= 0) & (offset < local_rows)
        plogit = jnp.sum(q_t * chosen, axis=0, keepdims=True)
        new_top = jnp.maximum(top, jnp.where(inside, plogit, very_low))
        total = total * jnp.exp(top - new_top) + jnp.where(inside, jnp.exp(plogit - new_top), 0.0)
        stat_ref[first + b, 0:1, :] = top
        stat_ref[first + b, 1:2, :] = new_top + jnp.log(total)
        stat_ref[first + b, 2:3, :] = jnp.where(inside, plogit, 0.0)
        stat_ref[first + b, 3:4, :] = jnp.where(inside, 1.0, 0.0)


def stats(messages, befores, items, at, loads):
    n = len(messages)
    rows, width = messages[0].shape[0] - EXTRA, messages[0].shape[1]
    total = n + sum(b.shape[0] for b in befores)
    sums = jax.ShapeDtypeStruct((n, width, rows), jnp.float32)
    held = [pltpu.VMEM(items.shape, jnp.float32)] if loads else []
    return pl.pallas_call(
        functools.partial(stats_kernel, n, len(befores), lax.axis_size("shard"), loads),
        out_shape=(sums, sums, jax.ShapeDtypeStruct((total, STAT, rows), jnp.float32), *held),
        in_specs=[smem] + [anywhere] * n + [vmem] * len(befores) + [hbm if loads else vmem],
        out_specs=(vmem, vmem, vmem, *[vmem] * len(held)),
        scratch_shapes=[
            *([pltpu.VMEM((KMAX, TILE, width), jnp.float32), pltpu.SemaphoreType.DMA((KMAX,))] if loads else []),
            pltpu.VMEM((n, rows + EXTRA, width), jnp.float32),
            pltpu.VMEM((rows, width), jnp.float32),
            pltpu.VMEM((n, EXTRA, width), jnp.int32),
            pltpu.SMEM((n, EXTRA, width), jnp.int32),
            pltpu.SemaphoreType.DMA((2, n)),
            pltpu.SemaphoreType.DMA((LOADS,)),
        ],
        compiler_params=pltpu.CompilerParams(vmem_limit_bytes=VMEM_LIMIT),
        cost_estimate=cost(5 * n),
        name="stats",
    )(at, *messages, *befores, items)


def dq_kernel(n, counts, *refs):
    stat_refs, refs = refs[:n], refs[n:]
    acc_refs, refs = refs[: len(counts)], refs[len(counts) :]
    chosen_refs, refs = refs[: len(counts)], refs[len(counts) :]
    loss_ref, term_ref, even_ref, odd_ref = refs
    b = 0
    for acc_ref, chosen_ref, count in zip(acc_refs, chosen_refs, counts):
        for i in range(count):
            parts = [stat_refs[j][b ^ j, 1:2, :] for j in range(n)]
            top = functools.reduce(jnp.maximum, parts)
            lse = top + jnp.log(sum(jnp.exp(p - top) for p in parts))
            plogit = sum(stat_refs[j][b ^ j, 2:3, :] for j in range(n))
            weight = jnp.exp(plogit - lse) - 1.0
            term_ref[0, b : b + 1, :] = lse
            term_ref[1, b : b + 1, :] = weight
            if b == 0:
                loss_ref[...] = lse - plogit
            own = stat_refs[0]
            share = acc_ref[i] * jnp.exp(own[b, 0:1, :] - lse) + chosen_ref[i] * (weight * own[b, 3:4, :])
            (odd_ref if b % 2 else even_ref)[b // 2] = share.T
            b += 1


def dq_shares(all_stats, accs, chosens):
    n, _, rows = all_stats[0].shape
    width = accs[0].shape[1]
    share = jax.ShapeDtypeStruct((n // 2, rows, width), jnp.float32)
    return pl.pallas_call(
        functools.partial(dq_kernel, n, [a.shape[0] for a in accs]),
        out_shape=(jax.ShapeDtypeStruct((1, rows), jnp.float32), jax.ShapeDtypeStruct((2, n, rows), jnp.float32), share, share),
        compiler_params=pltpu.CompilerParams(vmem_limit_bytes=VMEM_LIMIT),
        cost_estimate=cost(3),
        name="dq",
    )(*all_stats, *accs, *chosens)


def item_kernel(groups, n_shard, n_waits, is_first, is_last, at, *refs):
    n = sum(groups)
    weights, refs = refs[: len(groups)], refs[len(groups) :]
    msgs, refs = refs[:n], refs[n + n_waits :]
    lse_refs, refs = refs[: len(groups)], refs[len(groups) :]
    items, refs = refs[0], refs[1 if is_first else 2 :]
    acc, token, refs = refs[0], refs[1], refs[2:]
    if is_first:
        source, items, refs = items, refs[0], refs[1:]
    outs, refs = refs[: 2 * is_last], refs[2 * is_last :]
    q_ref, lse, whole, lists_ref, sems = refs
    rows, width = q_ref.shape[1] - EXTRA, q_ref.shape[2]
    span_rows = acc.shape[0]
    tiles = span_rows // TILE
    base, first_tile, core = at[1] + at[2] * TILE, at[2], at[3]
    chip = at[0] * at[4] + at[5]
    lists = Lists(lists_ref, rows, at[0], n_shard)
    get_lists = pltpu.make_async_copy(whole, lists_ref, sems.at[1, 0])

    def get_q(j):
        return pltpu.make_async_copy(msgs[j], q_ref.at[j], sems.at[0, j])

    for j in range(n):
        get_q(j).start()
    if is_first:
        start = pl.multiple_of(first_tile * TILE, TILE)
        get_items = pltpu.make_async_copy(source.at[pl.ds(start, span_rows)], items, sems.at[2, 0])
        get_items.start()
        acc[...] = jnp.zeros(acc.shape, jnp.float32)
    token[...] = jnp.zeros(token.shape, jnp.float32)
    for j in range(n):
        get_q(j).wait()
    whole[...] = q_ref[:, rows:, :].astype(jnp.int32)
    get_lists.start()
    get_lists.wait()

    def add_positives(b, weight, first):
        low, top = lists.bound(b, chip), lists.bound(b, chip + 1)

        @pl.loop(0, (top - low + STEP - 1) // STEP)
        def _(c):
            entries = [jnp.minimum(low + c * STEP + u, top - 1) for u in range(STEP)]
            rests = [jnp.where(low + c * STEP + u < top, 1.0, 0.0) for u in range(STEP)]
            heres = [lists.sorted_pos(b, i) - base for i in entries]
            places = [lists.place(b, i) for i in entries]
            olds = [acc[pl.ds(h, 1), :] for h in heres]
            terms = [q_ref[b, pl.ds(p, 1), :] * (weight[1, b - first, p] * r) for p, r in zip(places, rests)]
            for u in range(1, STEP):
                terms[u] = terms[u] + terms[u - 1] * jnp.where(heres[u] == heres[u - 1], 1.0, 0.0)
            for h, old, term in zip(heres, olds, terms):
                acc[pl.ds(h, 1), :] = old + term

    first = 0
    for size, weight, lse_ref in zip(groups, weights, lse_refs):
        lse[first : first + size, :] = lse_ref[0]
        pl.loop(first, first + size)(functools.partial(add_positives, weight=weight, first=first))
        first += size

    if is_first:
        get_items.wait()

    @pl.loop(0, n)
    def _(b):
        @pl.loop(0, lists.count(b))
        def _(k):
            tile = lists.tile(b, k) - first_tile

            @pl.when((tile >= 0) & (tile < tiles))
            def _():
                here = pl.ds(pl.multiple_of(tile * TILE, TILE), TILE)
                q = q_ref[b, :rows, :]
                logits = dot3(halves(items[here, :]), halves(q), ((1,), (1,)))
                prob = jnp.exp(logits - lse[pl.ds(b, 1), :])
                acc[here, :] += dot(prob, q)

    if is_last:
        own = span_rows // 2
        mine, other = outs
        put = [
            pltpu.make_async_copy(acc.at[pl.ds(pl.multiple_of((1 - core) * own, 8), own)], other, sems.at[2, 0]),
            pltpu.make_async_copy(acc.at[pl.ds(pl.multiple_of(core * own, 8), own)], mine, sems.at[2, 1]),
        ]
        for p in put:
            p.start()
        for p in put:
            p.wait()


def item_grads(groups, terms, items, acc, span_rows, at, is_last, waits=()):
    messages = [m for group in groups for m in group]
    n = len(messages)
    rows, width = messages[0].shape[0] - EXTRA, messages[0].shape[1]
    is_first = acc is None
    half = jax.ShapeDtypeStruct((span_rows // 2, width), jnp.float32)
    chips = pltpu.VMEM((span_rows, width), jnp.float32)
    token = jax.ShapeDtypeStruct((1, 128), jnp.float32)
    more = [chips] if is_first else [half, half] if is_last else []
    carried = [] if is_first else [acc]
    sizes = [len(group) for group in groups]
    return pl.pallas_call(
        functools.partial(item_kernel, sizes, lax.axis_size("shard"), len(waits), is_first, is_last),
        out_shape=(chips, token, *more),
        in_specs=[smem] * (1 + len(groups))
        + [anywhere] * (n + len(waits))
        + [vmem] * len(groups)
        + [hbm if is_first else vmem]
        + [vmem] * len(carried),
        out_specs=(vmem, vmem, *[vmem if is_first else anywhere] * len(more)),
        scratch_shapes=[
            pltpu.VMEM((n, rows + EXTRA, width), jnp.float32),
            pltpu.VMEM((n, rows), jnp.float32),
            pltpu.VMEM((n, EXTRA, width), jnp.int32),
            pltpu.SMEM((n, EXTRA, width), jnp.int32),
            pltpu.SemaphoreType.DMA((3, max(n, 2))),
        ],
        input_output_aliases={} if is_first else {2 + 2 * len(groups) + n + len(waits): 0},
        compiler_params=pltpu.CompilerParams(vmem_limit_bytes=VMEM_LIMIT),
        cost_estimate=cost(2 * n),
        name="item_grads",
    )(at, *terms, *messages, *waits, *terms, items, *carried)


def local(queries, items, positive, tile_ids, counts):
    dp_at, shard_at = lax.axis_index("dp"), lax.axis_index("shard")
    n_dp, n_shard = lax.axis_size("dp"), lax.axis_size("shard")
    rows, width = queries.shape
    local_rows = items.shape[0]
    span_rows = 2 * (local_rows // n_dp)
    n_chips = n_dp // 2
    chip_at = dp_at // 2
    at = jnp.stack([shard_at, shard_at * local_rows, chip_at * (span_rows // TILE), dp_at % 2, n_chips, chip_at])
    at = at.astype(jnp.int32)

    def top(j):
        return 1 << (j.bit_length() - 1)

    items = pltpu.with_memory_space_constraint(items, pltpu.HBM)
    queries = pltpu.with_memory_space_constraint(queries, pltpu.HBM)
    message = pack(queries, positive, tile_ids, counts, span_rows)
    own = [message] + [swap(message, "shard", j) for j in (1, 2)]
    straight = [message, None, swap(message, "dp", 4)]
    acc0, chosen0, stat0, held = stats([message], [], items, at, True)

    message, own[1], own[2], stat0 = together(message, own[1], own[2], stat0)
    straight[1] = swap(message, "dp", 2)
    for j in range(3, n_shard):
        own.append(swap(own[j ^ top(j)], "shard", top(j)))
    acc1, chosen1, stat1 = stats(own[1:3], [stat0], held, at, False)

    message, straight[2], stat1, *own[3:] = together(message, straight[2], stat1, *own[3:])
    straight += [swap(message, "dp", 2 * k) for k in range(3, n_chips)]
    far = {2: [straight[2]] + [swap(straight[2], "shard", j) for j in (1, 2)]}
    acc2, chosen2, stat = stats(own[3:], [stat1], held, at, False)

    all_stats = [stat]
    bit = 1
    while bit < n_shard:
        got = swap(jnp.stack(all_stats) if bit > 1 else stat, "shard", bit)
        all_stats += [got[j] for j in range(bit)] if bit > 1 else [got]
        bit *= 2
    all_stats[-1], far[2][1], far[2][2], straight[1], *straight[3:] = together(
        all_stats[-1], far[2][1], far[2][2], straight[1], *straight[3:]
    )
    loss, sent, even, odd = dq_shares(all_stats, [acc0, acc1, acc2], [chosen0, chosen1, chosen2])

    for k in range(3, n_chips):
        far[k] = [straight[k]] + [swap(straight[k], "shard", j) for j in (1, 2)]
    for j in range(3, n_shard):
        far[2].append(swap(far[2][j ^ top(j)], "shard", top(j)))
    grads, token, chip_items = item_grads([own], [sent], items, None, span_rows, at, False)
    near = [straight[1], swap(own[1], "dp", 2)]
    early = [token, near[1], far[2][3], *[m for k in range(3, n_chips) for m in far[k][1:]]]
    terms = [sent]
    bit = 1
    while bit < n_chips:
        got = swap(jnp.stack(terms) + none(*early) if bit > 1 else sent, "dp", 2 * bit)
        terms += [got[j] for j in range(bit)] if bit > 1 else [got]
        bit *= 2
    near += [swap(own[j] + none(terms[n_chips - 1]), "dp", 2) for j in range(2, n_shard)]
    for k in range(3, n_chips):
        for j in range(3, n_shard):
            far[k].append(swap(far[k][j ^ top(j)], "shard", top(j)))
    grads, token = item_grads([far[2]], [terms[2]], chip_items, grads, span_rows, at, False)[:2]

    shares = even + swap(odd, "shard", 1) + none(token)
    half_way = shares
    bit = 2
    while bit < n_shard:
        shares = shares[0::2] + swap(shares[1::2], "shard", bit)
        bit *= 2
    query_grad = shares[0]
    for k in range(3, n_chips):
        grads = item_grads([far[k]], [terms[k]], chip_items, grads, span_rows, at, False, [half_way, near[2]])[0]
    mine, other = item_grads([near], [terms[1]], chip_items, grads, span_rows, at, True, [query_grad])[2:]
    item_grad = mine + swap(other, "dp", 1)
    return loss.reshape(rows), query_grad, item_grad


def solution(mesh):
    placed = (
        P(("dp", "shard"), None),
        P("shard", None),
        P(("dp", "shard")),
        P(("dp", "shard"), None, None),
        P(("dp", "shard"), None),
    )
    return jax.shard_map(
        local,
        mesh=mesh,
        in_specs=placed,
        out_specs=(P(("dp", "shard")), P(("dp", "shard"), None), P(("shard", "dp"), None)),
        check_vma=False,
    )
```

```python
import functools

import jax
import jax.numpy as jnp
from jax import lax
from jax.experimental import pallas as pl
from jax.experimental.pallas import tpu as pltpu
from jax.sharding import PartitionSpec as P

TILE = 512
KMAX = 3
EXTRA = 8
LOADS = 8
GATHER = 8
STEP = 4
STAT = 4
MIB = 1024 * 1024
VMEM_LIMIT = 10 * MIB

very_low = -1e30
high, highest = lax.Precision.HIGH, lax.Precision.HIGHEST

smem = pl.BlockSpec(memory_space=pltpu.SMEM)
vmem = pl.BlockSpec(memory_space=pltpu.VMEM)
anywhere = pl.BlockSpec(memory_space=pl.ANY)
hbm = pl.BlockSpec(memory_space=pltpu.HBM)


def dot(a, b, dims=((1,), (0,)), precision=high):
    return lax.dot_general(a, b, (dims, ((), ())), precision=precision, preferred_element_type=jnp.float32)


def halves(x):
    upper = x.astype(jnp.bfloat16)
    return upper, (x - upper.astype(jnp.float32)).astype(jnp.bfloat16)


def dot3(a, b, dims=((1,), (0,))):
    def one(i, j):
        return lax.dot_general(a[i], b[j], (dims, ((), ())), preferred_element_type=jnp.float32)

    return (one(0, 1) + one(1, 0)) + one(0, 0)


def cost(us):
    return pl.CostEstimate(flops=0, bytes_accessed=int(us * 3.0e6), transcendentals=0)


def pack_kernel(step, ids_ref, counts_ref, q_ref, pos_ref, out_ref, sem):
    rows, width = q_ref.shape
    get_q = pltpu.make_async_copy(q_ref, out_ref.at[:rows], sem)
    get_q.start()
    out_ref[rows : rows + EXTRA, :] = jnp.zeros((EXTRA, width), jnp.float32)
    row = pos_ref[...].astype(jnp.float32)
    col = jnp.broadcast_to(row, (8, rows)).T[:, 0:1]
    at_row = lax.broadcasted_iota(jnp.int32, (rows, rows), 1)
    at_col = lax.broadcasted_iota(jnp.int32, (rows, rows), 0)
    before = (row < col) | ((row == col) & (at_row < at_col))
    rank = jnp.sum(before.astype(jnp.float32), axis=1, keepdims=True)
    placed = rank == at_row.astype(jnp.float32)
    sorted_pos = jnp.sum(jnp.where(placed, col, 0.0), axis=0, keepdims=True)
    sorted_at = jnp.sum(jnp.where(placed, at_col.astype(jnp.float32), 0.0), axis=0, keepdims=True)
    starts = lax.broadcasted_iota(jnp.int32, (rows, width), 1).astype(jnp.float32) * step
    bounds = jnp.sum((col < starts).astype(jnp.float32), axis=0, keepdims=True)
    lane = lax.broadcasted_iota(jnp.int32, (1, width), 1)
    lists = jnp.zeros((1, width), jnp.int32)
    n = counts_ref.shape[1]
    for i in range(n * KMAX):
        lists = jnp.where(lane == i, ids_ref[0, i // KMAX, i % KMAX], lists)
    for i in range(n):
        lists = jnp.where(lane == n * KMAX + i, counts_ref[0, i], lists)
    per = rows // width
    out_ref[rows + 3 * per : rows + 3 * per + 1, :] = lists.astype(jnp.float32)
    out_ref[rows + 3 * per + 1 : rows + 3 * per + 2, :] = bounds
    for first, values in ((0, row), (per, sorted_pos), (2 * per, sorted_at)):
        for i in range(per):
            out_ref[rows + first + i : rows + first + i + 1, :] = values[:, i * width : (i + 1) * width]
    get_q.wait()


def pack(queries, positive, tile_ids, counts, step):
    rows, width = queries.shape
    return pl.pallas_call(
        functools.partial(pack_kernel, float(step)),
        out_shape=jax.ShapeDtypeStruct((rows + EXTRA, width), jnp.float32),
        in_specs=[smem, smem, hbm, vmem],
        out_specs=vmem,
        scratch_shapes=[pltpu.SemaphoreType.DMA],
        compiler_params=pltpu.CompilerParams(vmem_limit_bytes=VMEM_LIMIT),
        cost_estimate=cost(2),
        name="pack",
    )(tile_ids, counts, queries, positive.reshape(1, rows))


class Lists:
    def __init__(self, ref, rows, shard_at, n_shard):
        self.ref, self.rows, self.shard_at, self.n_shard = ref, rows, shard_at, n_shard
        self.width = ref.shape[2]
        self.per = rows // self.width
        self.shift = self.width.bit_length() - 1

    def entry(self, b, first, i):
        return self.ref[b, first + (i >> self.shift), i & (self.width - 1)]

    def sorted_pos(self, b, i):
        return self.entry(b, self.per, i)

    def place(self, b, i):
        return self.entry(b, 2 * self.per, i)

    def tile(self, b, k):
        return self.ref[b, 3 * self.per, self.shard_at * KMAX + k]

    def count(self, b):
        return self.ref[b, 3 * self.per, self.n_shard * KMAX + self.shard_at]

    def bound(self, b, i):
        return self.ref[b, 3 * self.per + 1, i]


def swap(x, axis, bits):
    return lax.ppermute(x, axis, [(i, i ^ bits) for i in range(lax.axis_size(axis))])


def none(*xs):
    return sum(jnp.minimum(jnp.abs(x[(0,) * x.ndim]), 0.0) for x in xs)


def together(*xs):
    return lax.optimization_barrier(xs)


def stats_kernel(n, n_before, n_shard, loads, at, *refs):
    msgs, refs = refs[:n], refs[n:]
    befores, refs = refs[:n_before], refs[n_before:]
    source, acc_ref, chosen_ref, stat_ref, refs = refs[0], refs[1], refs[2], refs[3], refs[4:]
    items = source
    if loads:
        items, refs = refs[0], refs[1:]
    if loads:
        tiles, tile_sems, refs = refs[0], refs[1], refs[2:]
    q_ref, rowbuf, whole, lists_ref, sems, load_sems = refs
    rows = q_ref.shape[1] - EXTRA
    width = q_ref.shape[2]
    per = rows // width
    lists = Lists(lists_ref, rows, at[0], n_shard)
    base, local_rows = at[1], items.shape[0]
    chunk = local_rows // LOADS
    get_lists = pltpu.make_async_copy(whole, lists_ref, sems.at[1, 0])

    def get_q(j):
        return pltpu.make_async_copy(msgs[j], q_ref.at[j], sems.at[0, j])

    def get_items(i):
        part = pl.ds(i * chunk, chunk)
        return pltpu.make_async_copy(source.at[part], items.at[part], load_sems.at[i])

    def get_tile(k):
        start = pl.multiple_of(lists.tile(0, k) * TILE, TILE)
        return pltpu.make_async_copy(source.at[pl.ds(start, TILE)], tiles.at[k], tile_sems.at[k])

    for j in range(n):
        get_q(j).start()
    first = 0
    for before in befores:
        stat_ref[first : first + before.shape[0]] = before[...]
        first += before.shape[0]
    for j in range(n):
        get_q(j).wait()
    whole[...] = q_ref[:, rows:, :].astype(jnp.int32)
    get_lists.start()
    get_lists.wait()
    if loads:

        @pl.loop(0, lists.count(0))
        def _(k):
            get_tile(k).start()

        for i in range(LOADS):
            get_items(i).start()

    @pl.loop(0, n)
    def _(b):
        q_t = q_ref[b, :rows, :].T
        q_halves = halves(q_t)
        acc_ref[b] = jnp.zeros(acc_ref.shape[1:], jnp.float32)

        def visit(k, carry):
            top, total = carry
            if loads:
                get_tile(k).wait()
                tile = tiles[k]
            else:
                tile = items[pl.ds(pl.multiple_of(lists.tile(b, k) * TILE, TILE), TILE), :]
            logits = dot3(halves(tile), q_halves)
            new_top = jnp.maximum(top, jnp.max(logits, axis=0, keepdims=True))
            prob = jnp.exp(logits - new_top)
            scale = jnp.exp(top - new_top)
            total = total * scale + jnp.sum(prob, axis=0, keepdims=True)
            acc_ref[b] = acc_ref[b] * scale + dot(tile.T, prob)
            return new_top, total

        start = (jnp.full((1, rows), very_low, jnp.float32), jnp.zeros((1, rows), jnp.float32))
        top, total = lax.fori_loop(0, lists.count(b), visit, start)

        if loads:
            for i in range(LOADS):
                get_items(i).wait()
        rowbuf[...] = jnp.zeros(rowbuf.shape, jnp.float32)
        low, high_end = lists.bound(b, at[0] * at[4]), lists.bound(b, (at[0] + 1) * at[4])

        @pl.loop(0, (high_end - low + GATHER - 1) // GATHER)
        def _(c):
            entries = [jnp.minimum(low + c * GATHER + u, high_end - 1) for u in range(GATHER)]
            got = [items[pl.ds(lists.sorted_pos(b, i) - base, 1), :] for i in entries]
            for i, row in zip(entries, got):
                rowbuf[pl.ds(lists.place(b, i), 1), :] = row

        chosen = rowbuf[...].T
        chosen_ref[b] = chosen
        pos = jnp.concatenate([q_ref[b, rows + i : rows + i + 1, :] for i in range(per)], axis=1).astype(jnp.int32)
        offset = pos - base
        inside = (offset >= 0) & (offset < local_rows)
        plogit = jnp.sum(q_t * chosen, axis=0, keepdims=True)
        new_top = jnp.maximum(top, jnp.where(inside, plogit, very_low))
        total = total * jnp.exp(top - new_top) + jnp.where(inside, jnp.exp(plogit - new_top), 0.0)
        stat_ref[first + b, 0:1, :] = top
        stat_ref[first + b, 1:2, :] = new_top + jnp.log(total)
        stat_ref[first + b, 2:3, :] = jnp.where(inside, plogit, 0.0)
        stat_ref[first + b, 3:4, :] = jnp.where(inside, 1.0, 0.0)


def stats(messages, befores, items, at, loads):
    n = len(messages)
    rows, width = messages[0].shape[0] - EXTRA, messages[0].shape[1]
    total = n + sum(b.shape[0] for b in befores)
    sums = jax.ShapeDtypeStruct((n, width, rows), jnp.float32)
    held = [pltpu.VMEM(items.shape, jnp.float32)] if loads else []
    return pl.pallas_call(
        functools.partial(stats_kernel, n, len(befores), lax.axis_size("shard"), loads),
        out_shape=(sums, sums, jax.ShapeDtypeStruct((total, STAT, rows), jnp.float32), *held),
        in_specs=[smem] + [anywhere] * n + [vmem] * len(befores) + [hbm if loads else vmem],
        out_specs=(vmem, vmem, vmem, *[vmem] * len(held)),
        scratch_shapes=[
            *([pltpu.VMEM((KMAX, TILE, width), jnp.float32), pltpu.SemaphoreType.DMA((KMAX,))] if loads else []),
            pltpu.VMEM((n, rows + EXTRA, width), jnp.float32),
            pltpu.VMEM((rows, width), jnp.float32),
            pltpu.VMEM((n, EXTRA, width), jnp.int32),
            pltpu.SMEM((n, EXTRA, width), jnp.int32),
            pltpu.SemaphoreType.DMA((2, n)),
            pltpu.SemaphoreType.DMA((LOADS,)),
        ],
        compiler_params=pltpu.CompilerParams(vmem_limit_bytes=VMEM_LIMIT),
        cost_estimate=cost(5 * n),
        name="stats",
    )(at, *messages, *befores, items)


def dq_kernel(n, counts, *refs):
    stat_refs, refs = refs[:n], refs[n:]
    acc_refs, refs = refs[: len(counts)], refs[len(counts) :]
    chosen_refs, refs = refs[: len(counts)], refs[len(counts) :]
    loss_ref, term_ref, even_ref, odd_ref = refs
    b = 0
    for acc_ref, chosen_ref, count in zip(acc_refs, chosen_refs, counts):
        for i in range(count):
            parts = [stat_refs[j][b ^ j, 1:2, :] for j in range(n)]
            top = functools.reduce(jnp.maximum, parts)
            lse = top + jnp.log(sum(jnp.exp(p - top) for p in parts))
            plogit = sum(stat_refs[j][b ^ j, 2:3, :] for j in range(n))
            weight = jnp.exp(plogit - lse) - 1.0
            term_ref[0, b : b + 1, :] = lse
            term_ref[1, b : b + 1, :] = weight
            if b == 0:
                loss_ref[...] = lse - plogit
            own = stat_refs[0]
            share = acc_ref[i] * jnp.exp(own[b, 0:1, :] - lse) + chosen_ref[i] * (weight * own[b, 3:4, :])
            (odd_ref if b % 2 else even_ref)[b // 2] = share.T
            b += 1


def dq_shares(all_stats, accs, chosens):
    n, _, rows = all_stats[0].shape
    width = accs[0].shape[1]
    share = jax.ShapeDtypeStruct((n // 2, rows, width), jnp.float32)
    return pl.pallas_call(
        functools.partial(dq_kernel, n, [a.shape[0] for a in accs]),
        out_shape=(jax.ShapeDtypeStruct((1, rows), jnp.float32), jax.ShapeDtypeStruct((2, n, rows), jnp.float32), share, share),
        compiler_params=pltpu.CompilerParams(vmem_limit_bytes=VMEM_LIMIT),
        cost_estimate=cost(3),
        name="dq",
    )(*all_stats, *accs, *chosens)


def item_kernel(groups, n_shard, n_waits, n_through, is_first, is_last, at, *refs):
    n = sum(size for size, _ in groups)
    weights, refs = refs[: len(groups)], refs[len(groups) :]
    msgs, refs = refs[:n], refs[n + n_waits :]
    lse_refs, refs = refs[: len(groups)], refs[len(groups) :]
    items, refs = refs[0], refs[1 if is_first else 2 :]
    acc, token, refs = refs[0], refs[1], refs[2:]
    if is_first:
        source, items, refs = items, refs[0], refs[1:]
    outs, refs = refs[: 2 * is_last], refs[2 * is_last + n_through :]
    q_ref, lse, whole, lists_ref, sems = refs
    rows, width = q_ref.shape[1] - EXTRA, q_ref.shape[2]
    span_rows = acc.shape[0]
    tiles = span_rows // TILE
    base, first_tile, core = at[1] + at[2] * TILE, at[2], at[3]
    chip = at[0] * at[4] + at[5]
    lists = Lists(lists_ref, rows, at[0], n_shard)
    get_lists = pltpu.make_async_copy(whole, lists_ref, sems.at[1, 0])

    def get_q(j):
        return pltpu.make_async_copy(msgs[j], q_ref.at[j], sems.at[0, j])

    for j in range(n):
        get_q(j).start()
    if is_first:
        start = pl.multiple_of(first_tile * TILE, TILE)
        get_items = pltpu.make_async_copy(source.at[pl.ds(start, span_rows)], items, sems.at[2, 0])
        get_items.start()
        acc[...] = jnp.zeros(acc.shape, jnp.float32)
    token[...] = jnp.zeros(token.shape, jnp.float32)
    for j in range(n):
        get_q(j).wait()
    whole[...] = q_ref[:, rows:, :].astype(jnp.int32)
    get_lists.start()
    get_lists.wait()

    def add_positives(b, weight, first):
        low, top = lists.bound(b, chip), lists.bound(b, chip + 1)

        @pl.loop(0, (top - low + STEP - 1) // STEP)
        def _(c):
            entries = [jnp.minimum(low + c * STEP + u, top - 1) for u in range(STEP)]
            rests = [jnp.where(low + c * STEP + u < top, 1.0, 0.0) for u in range(STEP)]
            heres = [lists.sorted_pos(b, i) - base for i in entries]
            places = [lists.place(b, i) for i in entries]
            olds = [acc[pl.ds(h, 1), :] for h in heres]
            terms = [q_ref[b, pl.ds(p, 1), :] * (weight[1, b - first, p] * r) for p, r in zip(places, rests)]
            for u in range(1, STEP):
                terms[u] = terms[u] + terms[u - 1] * jnp.where(heres[u] == heres[u - 1], 1.0, 0.0)
            for h, old, term in zip(heres, olds, terms):
                acc[pl.ds(h, 1), :] = old + term

    first = 0
    for (size, begin), weight, lse_ref in zip(groups, weights, lse_refs):
        lse[first : first + size, :] = lse_ref[0, begin : begin + size, :]
        pl.loop(first, first + size)(functools.partial(add_positives, weight=weight, first=first - begin))
        first += size

    if is_first:
        get_items.wait()

    @pl.loop(0, n)
    def _(b):
        @pl.loop(0, lists.count(b))
        def _(k):
            tile = lists.tile(b, k) - first_tile

            @pl.when((tile >= 0) & (tile < tiles))
            def _():
                here = pl.ds(pl.multiple_of(tile * TILE, TILE), TILE)
                q = q_ref[b, :rows, :]
                logits = dot3(halves(items[here, :]), halves(q), ((1,), (1,)))
                prob = jnp.exp(logits - lse[pl.ds(b, 1), :])
                acc[here, :] += dot(prob, q)

    if is_last:
        own = span_rows // 2
        mine, other = outs
        put = [
            pltpu.make_async_copy(acc.at[pl.ds(pl.multiple_of((1 - core) * own, 8), own)], other, sems.at[2, 0]),
            pltpu.make_async_copy(acc.at[pl.ds(pl.multiple_of(core * own, 8), own)], mine, sems.at[2, 1]),
        ]
        for p in put:
            p.start()
        for p in put:
            p.wait()


def item_grads(groups, terms, items, acc, span_rows, at, is_last, waits=(), through=()):
    waits = [*waits, *through]
    messages = [m for group, _ in groups for m in group]
    n = len(messages)
    rows, width = messages[0].shape[0] - EXTRA, messages[0].shape[1]
    is_first = acc is None
    half = jax.ShapeDtypeStruct((span_rows // 2, width), jnp.float32)
    chips = pltpu.VMEM((span_rows, width), jnp.float32)
    token = jax.ShapeDtypeStruct((1, 128), jnp.float32)
    more = [chips] if is_first else [half, half] if is_last else []
    carried = [] if is_first else [acc]
    sizes = [(len(group), begin) for group, begin in groups]
    return pl.pallas_call(
        functools.partial(item_kernel, sizes, lax.axis_size("shard"), len(waits), len(through), is_first, is_last),
        out_shape=(chips, token, *more, *[jax.ShapeDtypeStruct(x.shape, x.dtype) for x in through]),
        in_specs=[smem] * (1 + len(groups))
        + [anywhere] * (n + len(waits))
        + [vmem] * len(groups)
        + [hbm if is_first else vmem]
        + [vmem] * len(carried),
        out_specs=(vmem, vmem, *[vmem if is_first else anywhere] * len(more), *[anywhere] * len(through)),
        scratch_shapes=[
            pltpu.VMEM((n, rows + EXTRA, width), jnp.float32),
            pltpu.VMEM((n, rows), jnp.float32),
            pltpu.VMEM((n, EXTRA, width), jnp.int32),
            pltpu.SMEM((n, EXTRA, width), jnp.int32),
            pltpu.SemaphoreType.DMA((3, max(n, 2))),
        ],
        input_output_aliases={
            **({} if is_first else {2 + 2 * len(groups) + n + len(waits): 0}),
            **{1 + len(groups) + n + len(waits) - len(through) + i: 2 + len(more) + i for i in range(len(through))},
        },
        compiler_params=pltpu.CompilerParams(vmem_limit_bytes=VMEM_LIMIT + max(n - 4, 0) * MIB),
        cost_estimate=cost(2 * n),
        name="item_grads",
    )(at, *terms, *messages, *waits, *terms, items, *carried)


def local(queries, items, positive, tile_ids, counts):
    dp_at, shard_at = lax.axis_index("dp"), lax.axis_index("shard")
    n_dp, n_shard = lax.axis_size("dp"), lax.axis_size("shard")
    rows, width = queries.shape
    local_rows = items.shape[0]
    span_rows = 2 * (local_rows // n_dp)
    n_chips = n_dp // 2
    chip_at = dp_at // 2
    at = jnp.stack([shard_at, shard_at * local_rows, chip_at * (span_rows // TILE), dp_at % 2, n_chips, chip_at])
    at = at.astype(jnp.int32)

    def top(j):
        return 1 << (j.bit_length() - 1)

    items = pltpu.with_memory_space_constraint(items, pltpu.HBM)
    queries = pltpu.with_memory_space_constraint(queries, pltpu.HBM)
    message = pack(queries, positive, tile_ids, counts, span_rows)
    own = [message] + [swap(message, "shard", j) for j in (1, 2)]
    straight = [message, None, swap(message, "dp", 4)]
    acc0, chosen0, stat0, held = stats([message], [], items, at, True)

    message, own[1], own[2], stat0 = together(message, own[1], own[2], stat0)
    straight[1] = swap(message, "dp", 2)
    for j in range(3, n_shard):
        own.append(swap(own[j ^ top(j)], "shard", top(j)))
    acc1, chosen1, stat1 = stats(own[1:3], [stat0], held, at, False)

    message, straight[2], stat1, *own[3:] = together(message, straight[2], stat1, *own[3:])
    straight += [swap(message, "dp", 2 * k) for k in range(3, n_chips)]
    far = {2: [straight[2]] + [swap(straight[2], "shard", j) for j in (1, 2)]}
    acc2, chosen2, stat = stats(own[3:], [stat1], held, at, False)

    all_stats = [stat]
    bit = 1
    while bit < n_shard:
        got = swap(jnp.stack(all_stats) if bit > 1 else stat, "shard", bit)
        all_stats += [got[j] for j in range(bit)] if bit > 1 else [got]
        bit *= 2
    all_stats[-1], far[2][1], far[2][2], straight[1], *straight[3:] = together(
        all_stats[-1], far[2][1], far[2][2], straight[1], *straight[3:]
    )
    loss, sent, even, odd = dq_shares(all_stats, [acc0, acc1, acc2], [chosen0, chosen1, chosen2])

    for k in range(3, n_chips):
        far[k] = [straight[k]] + [swap(straight[k], "shard", j) for j in (1, 2)]
    for j in range(3, n_shard):
        far[2].append(swap(far[2][j ^ top(j)], "shard", top(j)))
    grads, token, chip_items, odd = item_grads([(own, 0)], [sent], items, None, span_rows, at, False, through=[odd])
    near = [straight[1], swap(own[1], "dp", 2)]
    early = [token, near[1], *[m for k in range(3, n_chips) for m in far[k][1:]]]
    terms = [sent]
    bit = 1
    while bit < n_chips:
        got = swap(jnp.stack(terms) + none(*early) if bit > 1 else sent, "dp", 2 * bit)
        terms += [got[j] for j in range(bit)] if bit > 1 else [got]
        bit *= 2
    near += [swap(own[j] + none(terms[n_chips - 1]), "dp", 2) for j in range(2, n_shard)]
    for k in range(3, n_chips):
        for j in range(3, n_shard):
            far[k].append(swap(far[k][j ^ top(j)], "shard", top(j)))
    grads, token = item_grads([(far[2], 0)], [terms[2]], chip_items, grads, span_rows, at, False)[:2]

    shares = even + swap(odd, "shard", 1) + none(token)
    half_way = shares
    bit = 2
    while bit < n_shard:
        shares = shares[0::2] + swap(shares[1::2], "shard", bit)
        bit *= 2
    query_grad = shares[0]
    for k in range(3, n_chips - 1):
        grads = item_grads([(far[k], 0)], [terms[k]], chip_items, grads, span_rows, at, False)[0]
    k = n_chips - 1
    most = [(far[k], 0), (near[: n_shard - 1], 0)]
    grads = item_grads(most, [terms[k], terms[1]], chip_items, grads, span_rows, at, False, [half_way])[0]
    rest = [(near[n_shard - 1 :], n_shard - 1)]
    mine, other = item_grads(rest, [terms[1]], chip_items, grads, span_rows, at, True, [query_grad])[2:]
    item_grad = mine + swap(other, "dp", 1)
    return loss.reshape(rows), query_grad, item_grad


def solution(mesh):
    placed = (
        P(("dp", "shard"), None),
        P("shard", None),
        P(("dp", "shard")),
        P(("dp", "shard"), None, None),
        P(("dp", "shard"), None),
    )
    return jax.shard_map(
        local,
        mesh=mesh,
        in_specs=placed,
        out_specs=(P(("dp", "shard")), P(("dp", "shard"), None), P(("shard", "dp"), None)),
        check_vma=False,
    )
```

```python
import functools

import jax
import jax.numpy as jnp
from jax import lax
from jax.experimental import pallas as pl
from jax.experimental.pallas import tpu as pltpu
from jax.sharding import PartitionSpec as P

TILE = 512
KMAX = 3
EXTRA = 8
LOADS = 8
GATHER = 8
STEP = 4
STAT = 4
MIB = 1024 * 1024
VMEM_LIMIT = 10 * MIB

very_low = -1e30
high, highest = lax.Precision.HIGH, lax.Precision.HIGHEST

smem = pl.BlockSpec(memory_space=pltpu.SMEM)
vmem = pl.BlockSpec(memory_space=pltpu.VMEM)
anywhere = pl.BlockSpec(memory_space=pl.ANY)
hbm = pl.BlockSpec(memory_space=pltpu.HBM)


def dot(a, b, dims=((1,), (0,)), precision=high):
    return lax.dot_general(a, b, (dims, ((), ())), precision=precision, preferred_element_type=jnp.float32)


def halves(x):
    upper = x.astype(jnp.bfloat16)
    return upper, (x - upper.astype(jnp.float32)).astype(jnp.bfloat16)


def dot3(a, b, dims=((1,), (0,))):
    def one(i, j):
        return lax.dot_general(a[i], b[j], (dims, ((), ())), preferred_element_type=jnp.float32)

    return (one(0, 1) + one(1, 0)) + one(0, 0)


def cost(us):
    return pl.CostEstimate(flops=0, bytes_accessed=int(us * 3.0e6), transcendentals=0)


def pack_kernel(step, ids_ref, counts_ref, q_ref, pos_ref, out_ref, sem):
    rows, width = q_ref.shape
    get_q = pltpu.make_async_copy(q_ref, out_ref.at[:rows], sem)
    get_q.start()
    out_ref[rows : rows + EXTRA, :] = jnp.zeros((EXTRA, width), jnp.float32)
    row = pos_ref[...].astype(jnp.float32)
    col = jnp.broadcast_to(row, (8, rows)).T[:, 0:1]
    at_row = lax.broadcasted_iota(jnp.int32, (rows, rows), 1)
    at_col = lax.broadcasted_iota(jnp.int32, (rows, rows), 0)
    before = (row < col) | ((row == col) & (at_row < at_col))
    rank = jnp.sum(before.astype(jnp.float32), axis=1, keepdims=True)
    placed = rank == at_row.astype(jnp.float32)
    sorted_pos = jnp.sum(jnp.where(placed, col, 0.0), axis=0, keepdims=True)
    sorted_at = jnp.sum(jnp.where(placed, at_col.astype(jnp.float32), 0.0), axis=0, keepdims=True)
    starts = lax.broadcasted_iota(jnp.int32, (rows, width), 1).astype(jnp.float32) * step
    bounds = jnp.sum((col < starts).astype(jnp.float32), axis=0, keepdims=True)
    lane = lax.broadcasted_iota(jnp.int32, (1, width), 1)
    lists = jnp.zeros((1, width), jnp.int32)
    n = counts_ref.shape[1]
    for i in range(n * KMAX):
        lists = jnp.where(lane == i, ids_ref[0, i // KMAX, i % KMAX], lists)
    for i in range(n):
        lists = jnp.where(lane == n * KMAX + i, counts_ref[0, i], lists)
    per = rows // width
    out_ref[rows + 3 * per : rows + 3 * per + 1, :] = lists.astype(jnp.float32)
    out_ref[rows + 3 * per + 1 : rows + 3 * per + 2, :] = bounds
    for first, values in ((0, row), (per, sorted_pos), (2 * per, sorted_at)):
        for i in range(per):
            out_ref[rows + first + i : rows + first + i + 1, :] = values[:, i * width : (i + 1) * width]
    get_q.wait()


def pack(queries, positive, tile_ids, counts, step):
    rows, width = queries.shape
    return pl.pallas_call(
        functools.partial(pack_kernel, float(step)),
        out_shape=jax.ShapeDtypeStruct((rows + EXTRA, width), jnp.float32),
        in_specs=[smem, smem, hbm, vmem],
        out_specs=vmem,
        scratch_shapes=[pltpu.SemaphoreType.DMA],
        compiler_params=pltpu.CompilerParams(vmem_limit_bytes=VMEM_LIMIT),
        cost_estimate=cost(2),
        name="pack",
    )(tile_ids, counts, queries, positive.reshape(1, rows))


class Lists:
    def __init__(self, ref, rows, shard_at, n_shard):
        self.ref, self.rows, self.shard_at, self.n_shard = ref, rows, shard_at, n_shard
        self.width = ref.shape[2]
        self.per = rows // self.width
        self.shift = self.width.bit_length() - 1

    def entry(self, b, first, i):
        return self.ref[b, first + (i >> self.shift), i & (self.width - 1)]

    def sorted_pos(self, b, i):
        return self.entry(b, self.per, i)

    def place(self, b, i):
        return self.entry(b, 2 * self.per, i)

    def tile(self, b, k):
        return self.ref[b, 3 * self.per, self.shard_at * KMAX + k]

    def count(self, b):
        return self.ref[b, 3 * self.per, self.n_shard * KMAX + self.shard_at]

    def bound(self, b, i):
        return self.ref[b, 3 * self.per + 1, i]


def swap(x, axis, bits):
    return lax.ppermute(x, axis, [(i, i ^ bits) for i in range(lax.axis_size(axis))])


def none(*xs):
    return sum(jnp.minimum(jnp.abs(x[(0,) * x.ndim]), 0.0) for x in xs)


def together(*xs):
    return lax.optimization_barrier(xs)


def stats_kernel(n, n_before, n_shard, loads, at, *refs):
    msgs, refs = refs[:n], refs[n:]
    befores, refs = refs[:n_before], refs[n_before:]
    source, acc_ref, chosen_ref, stat_ref, refs = refs[0], refs[1], refs[2], refs[3], refs[4:]
    items = source
    if loads:
        items, refs = refs[0], refs[1:]
    if loads:
        tiles, tile_sems, refs = refs[0], refs[1], refs[2:]
    q_ref, rowbuf, whole, meta, lists_ref, sems, load_sems = refs
    rows = q_ref.shape[1] - EXTRA
    width = q_ref.shape[2]
    per = rows // width
    lists = Lists(lists_ref, rows, at[0], n_shard)
    base, local_rows = at[1], items.shape[0]
    chunk = local_rows // LOADS
    get_lists = pltpu.make_async_copy(whole, lists_ref, sems.at[1, 0])

    def get_meta(j):
        return pltpu.make_async_copy(msgs[j].at[rows : rows + EXTRA], meta.at[j], sems.at[2, j])

    def get_q(j):
        return pltpu.make_async_copy(msgs[j], q_ref.at[j], sems.at[0, j])

    def get_items(i):
        part = pl.ds(i * chunk, chunk)
        return pltpu.make_async_copy(source.at[part], items.at[part], load_sems.at[i])

    def get_tile(k):
        start = pl.multiple_of(lists.tile(0, k) * TILE, TILE)
        return pltpu.make_async_copy(source.at[pl.ds(start, TILE)], tiles.at[k], tile_sems.at[k])

    for j in range(n):
        get_meta(j).start()
    for j in range(n):
        get_q(j).start()
    if loads:
        for i in range(LOADS // 2):
            get_items(i).start()
    first = 0
    for before in befores:
        stat_ref[first : first + before.shape[0]] = before[...]
        first += before.shape[0]
    for j in range(n):
        get_meta(j).wait()
    whole[...] = meta[...].astype(jnp.int32)
    get_lists.start()
    for j in range(n):
        get_q(j).wait()
    get_lists.wait()
    if loads:

        @pl.loop(0, lists.count(0))
        def _(k):
            get_tile(k).start()

        for i in range(LOADS // 2, LOADS):
            get_items(i).start()

    @pl.loop(0, n)
    def _(b):
        q_t = q_ref[b, :rows, :].T
        q_halves = halves(q_t)
        acc_ref[b] = jnp.zeros(acc_ref.shape[1:], jnp.float32)

        def visit(k, carry):
            top, total = carry
            if loads:
                get_tile(k).wait()
                tile = tiles[k]
            else:
                tile = items[pl.ds(pl.multiple_of(lists.tile(b, k) * TILE, TILE), TILE), :]
            logits = dot3(halves(tile), q_halves)
            new_top = jnp.maximum(top, jnp.max(logits, axis=0, keepdims=True))
            prob = jnp.exp(logits - new_top)
            scale = jnp.exp(top - new_top)
            total = total * scale + jnp.sum(prob, axis=0, keepdims=True)
            acc_ref[b] = acc_ref[b] * scale + dot(tile.T, prob)
            return new_top, total

        start = (jnp.full((1, rows), very_low, jnp.float32), jnp.zeros((1, rows), jnp.float32))
        top, total = lax.fori_loop(0, lists.count(b), visit, start)

        if loads:
            for i in range(LOADS):
                get_items(i).wait()
        rowbuf[...] = jnp.zeros(rowbuf.shape, jnp.float32)
        low, high_end = lists.bound(b, at[0] * at[4]), lists.bound(b, (at[0] + 1) * at[4])

        @pl.loop(0, (high_end - low + GATHER - 1) // GATHER)
        def _(c):
            entries = [jnp.minimum(low + c * GATHER + u, high_end - 1) for u in range(GATHER)]
            got = [items[pl.ds(lists.sorted_pos(b, i) - base, 1), :] for i in entries]
            for i, row in zip(entries, got):
                rowbuf[pl.ds(lists.place(b, i), 1), :] = row

        chosen = rowbuf[...].T
        chosen_ref[b] = chosen
        pos = jnp.concatenate([q_ref[b, rows + i : rows + i + 1, :] for i in range(per)], axis=1).astype(jnp.int32)
        offset = pos - base
        inside = (offset >= 0) & (offset < local_rows)
        plogit = jnp.sum(q_t * chosen, axis=0, keepdims=True)
        new_top = jnp.maximum(top, jnp.where(inside, plogit, very_low))
        total = total * jnp.exp(top - new_top) + jnp.where(inside, jnp.exp(plogit - new_top), 0.0)
        stat_ref[first + b, 0:1, :] = top
        stat_ref[first + b, 1:2, :] = new_top + jnp.log(total)
        stat_ref[first + b, 2:3, :] = jnp.where(inside, plogit, 0.0)
        stat_ref[first + b, 3:4, :] = jnp.where(inside, 1.0, 0.0)


def stats(messages, befores, items, at, loads):
    n = len(messages)
    rows, width = messages[0].shape[0] - EXTRA, messages[0].shape[1]
    total = n + sum(b.shape[0] for b in befores)
    sums = jax.ShapeDtypeStruct((n, width, rows), jnp.float32)
    held = [pltpu.VMEM(items.shape, jnp.float32)] if loads else []
    return pl.pallas_call(
        functools.partial(stats_kernel, n, len(befores), lax.axis_size("shard"), loads),
        out_shape=(sums, sums, jax.ShapeDtypeStruct((total, STAT, rows), jnp.float32), *held),
        in_specs=[smem] + [anywhere] * n + [vmem] * len(befores) + [hbm if loads else vmem],
        out_specs=(vmem, vmem, vmem, *[vmem] * len(held)),
        scratch_shapes=[
            *([pltpu.VMEM((KMAX, TILE, width), jnp.float32), pltpu.SemaphoreType.DMA((KMAX,))] if loads else []),
            pltpu.VMEM((n, rows + EXTRA, width), jnp.float32),
            pltpu.VMEM((rows, width), jnp.float32),
            pltpu.VMEM((n, EXTRA, width), jnp.int32),
            pltpu.VMEM((n, EXTRA, width), jnp.float32),
            pltpu.SMEM((n, EXTRA, width), jnp.int32),
            pltpu.SemaphoreType.DMA((3, n)),
            pltpu.SemaphoreType.DMA((LOADS,)),
        ],
        compiler_params=pltpu.CompilerParams(vmem_limit_bytes=VMEM_LIMIT),
        cost_estimate=cost(5 * n),
        name="stats",
    )(at, *messages, *befores, items)


def dq_kernel(n, counts, *refs):
    stat_refs, refs = refs[:n], refs[n:]
    acc_refs, refs = refs[: len(counts)], refs[len(counts) :]
    chosen_refs, refs = refs[: len(counts)], refs[len(counts) :]
    loss_ref, term_ref, even_ref, odd_ref = refs
    b = 0
    for acc_ref, chosen_ref, count in zip(acc_refs, chosen_refs, counts):
        for i in range(count):
            parts = [stat_refs[j][b ^ j, 1:2, :] for j in range(n)]
            top = functools.reduce(jnp.maximum, parts)
            lse = top + jnp.log(sum(jnp.exp(p - top) for p in parts))
            plogit = sum(stat_refs[j][b ^ j, 2:3, :] for j in range(n))
            weight = jnp.exp(plogit - lse) - 1.0
            term_ref[0, b : b + 1, :] = lse
            term_ref[1, b : b + 1, :] = weight
            if b == 0:
                loss_ref[...] = lse - plogit
            own = stat_refs[0]
            share = acc_ref[i] * jnp.exp(own[b, 0:1, :] - lse) + chosen_ref[i] * (weight * own[b, 3:4, :])
            (odd_ref if b % 2 else even_ref)[b // 2] = share.T
            b += 1


def dq_shares(all_stats, accs, chosens):
    n, _, rows = all_stats[0].shape
    width = accs[0].shape[1]
    share = jax.ShapeDtypeStruct((n // 2, rows, width), jnp.float32)
    return pl.pallas_call(
        functools.partial(dq_kernel, n, [a.shape[0] for a in accs]),
        out_shape=(jax.ShapeDtypeStruct((1, rows), jnp.float32), jax.ShapeDtypeStruct((2, n, rows), jnp.float32), share, share),
        compiler_params=pltpu.CompilerParams(vmem_limit_bytes=VMEM_LIMIT),
        cost_estimate=cost(3),
        name="dq",
    )(*all_stats, *accs, *chosens)


def item_kernel(groups, n_shard, n_waits, n_through, is_first, is_last, at, *refs):
    n = sum(size for size, _ in groups)
    weights, refs = refs[: len(groups)], refs[len(groups) :]
    msgs, refs = refs[:n], refs[n + n_waits :]
    lse_refs, refs = refs[: len(groups)], refs[len(groups) :]
    items, refs = refs[0], refs[1 if is_first else 2 :]
    acc, token, refs = refs[0], refs[1], refs[2:]
    if is_first:
        source, items, refs = items, refs[0], refs[1:]
    outs, refs = refs[: 2 * is_last], refs[2 * is_last + n_through :]
    q_ref, lse, whole, meta, lists_ref, sems = refs
    rows, width = q_ref.shape[1] - EXTRA, q_ref.shape[2]
    span_rows = acc.shape[0]
    tiles = span_rows // TILE
    base, first_tile, core = at[1] + at[2] * TILE, at[2], at[3]
    chip = at[0] * at[4] + at[5]
    lists = Lists(lists_ref, rows, at[0], n_shard)
    get_lists = pltpu.make_async_copy(whole, lists_ref, sems.at[1, 0])

    def get_meta(j):
        return pltpu.make_async_copy(msgs[j].at[rows : rows + EXTRA], meta.at[j], sems.at[3, j])

    def get_q(j):
        return pltpu.make_async_copy(msgs[j], q_ref.at[j], sems.at[0, j])

    for j in range(n):
        get_meta(j).start()
    for j in range(n):
        get_q(j).start()
    if is_first:
        start = pl.multiple_of(first_tile * TILE, TILE)
        get_items = pltpu.make_async_copy(source.at[pl.ds(start, span_rows)], items, sems.at[2, 0])
        get_items.start()
        acc[...] = jnp.zeros(acc.shape, jnp.float32)
    token[...] = jnp.zeros(token.shape, jnp.float32)
    for j in range(n):
        get_meta(j).wait()
    whole[...] = meta[...].astype(jnp.int32)
    get_lists.start()
    for j in range(n):
        get_q(j).wait()
    get_lists.wait()

    def add_positives(b, weight, first):
        low, top = lists.bound(b, chip), lists.bound(b, chip + 1)

        @pl.loop(0, (top - low + STEP - 1) // STEP)
        def _(c):
            entries = [jnp.minimum(low + c * STEP + u, top - 1) for u in range(STEP)]
            rests = [jnp.where(low + c * STEP + u < top, 1.0, 0.0) for u in range(STEP)]
            heres = [lists.sorted_pos(b, i) - base for i in entries]
            places = [lists.place(b, i) for i in entries]
            olds = [acc[pl.ds(h, 1), :] for h in heres]
            terms = [q_ref[b, pl.ds(p, 1), :] * (weight[1, b - first, p] * r) for p, r in zip(places, rests)]
            for u in range(1, STEP):
                terms[u] = terms[u] + terms[u - 1] * jnp.where(heres[u] == heres[u - 1], 1.0, 0.0)
            for h, old, term in zip(heres, olds, terms):
                acc[pl.ds(h, 1), :] = old + term

    first = 0
    for (size, begin), weight, lse_ref in zip(groups, weights, lse_refs):
        lse[first : first + size, :] = lse_ref[0, begin : begin + size, :]
        pl.loop(first, first + size)(functools.partial(add_positives, weight=weight, first=first - begin))
        first += size

    if is_first:
        get_items.wait()

    @pl.loop(0, n)
    def _(b):
        @pl.loop(0, lists.count(b))
        def _(k):
            tile = lists.tile(b, k) - first_tile

            @pl.when((tile >= 0) & (tile < tiles))
            def _():
                here = pl.ds(pl.multiple_of(tile * TILE, TILE), TILE)
                q = q_ref[b, :rows, :]
                logits = dot3(halves(items[here, :]), halves(q), ((1,), (1,)))
                prob = jnp.exp(logits - lse[pl.ds(b, 1), :])
                acc[here, :] += dot(prob, q)

    if is_last:
        own = span_rows // 2
        mine, other = outs
        put = [
            pltpu.make_async_copy(acc.at[pl.ds(pl.multiple_of((1 - core) * own, 8), own)], other, sems.at[2, 0]),
            pltpu.make_async_copy(acc.at[pl.ds(pl.multiple_of(core * own, 8), own)], mine, sems.at[2, 1]),
        ]
        for p in put:
            p.start()
        for p in put:
            p.wait()


def item_grads(groups, terms, items, acc, span_rows, at, is_last, waits=(), through=()):
    waits = [*waits, *through]
    messages = [m for group, _ in groups for m in group]
    n = len(messages)
    rows, width = messages[0].shape[0] - EXTRA, messages[0].shape[1]
    is_first = acc is None
    half = jax.ShapeDtypeStruct((span_rows // 2, width), jnp.float32)
    chips = pltpu.VMEM((span_rows, width), jnp.float32)
    token = jax.ShapeDtypeStruct((1, 128), jnp.float32)
    more = [chips] if is_first else [half, half] if is_last else []
    carried = [] if is_first else [acc]
    sizes = [(len(group), begin) for group, begin in groups]
    return pl.pallas_call(
        functools.partial(item_kernel, sizes, lax.axis_size("shard"), len(waits), len(through), is_first, is_last),
        out_shape=(chips, token, *more, *[jax.ShapeDtypeStruct(x.shape, x.dtype) for x in through]),
        in_specs=[smem] * (1 + len(groups))
        + [anywhere] * (n + len(waits))
        + [vmem] * len(groups)
        + [hbm if is_first else vmem]
        + [vmem] * len(carried),
        out_specs=(vmem, vmem, *[vmem if is_first else anywhere] * len(more), *[anywhere] * len(through)),
        scratch_shapes=[
            pltpu.VMEM((n, rows + EXTRA, width), jnp.float32),
            pltpu.VMEM((n, rows), jnp.float32),
            pltpu.VMEM((n, EXTRA, width), jnp.int32),
            pltpu.VMEM((n, EXTRA, width), jnp.float32),
            pltpu.SMEM((n, EXTRA, width), jnp.int32),
            pltpu.SemaphoreType.DMA((4, max(n, 2))),
        ],
        input_output_aliases={
            **({} if is_first else {2 + 2 * len(groups) + n + len(waits): 0}),
            **{1 + len(groups) + n + len(waits) - len(through) + i: 2 + len(more) + i for i in range(len(through))},
        },
        compiler_params=pltpu.CompilerParams(vmem_limit_bytes=VMEM_LIMIT + max(n - 4, 0) * MIB),
        cost_estimate=cost(2 * n),
        name="item_grads",
    )(at, *terms, *messages, *waits, *terms, items, *carried)


def local(queries, items, positive, tile_ids, counts):
    dp_at, shard_at = lax.axis_index("dp"), lax.axis_index("shard")
    n_dp, n_shard = lax.axis_size("dp"), lax.axis_size("shard")
    rows, width = queries.shape
    local_rows = items.shape[0]
    span_rows = 2 * (local_rows // n_dp)
    n_chips = n_dp // 2
    chip_at = dp_at // 2
    at = jnp.stack([shard_at, shard_at * local_rows, chip_at * (span_rows // TILE), dp_at % 2, n_chips, chip_at])
    at = at.astype(jnp.int32)

    def top(j):
        return 1 << (j.bit_length() - 1)

    items = pltpu.with_memory_space_constraint(items, pltpu.HBM)
    queries = pltpu.with_memory_space_constraint(queries, pltpu.HBM)
    message = pack(queries, positive, tile_ids, counts, span_rows)
    own = [message] + [swap(message, "shard", j) for j in (1, 2)]
    straight = [message, None, swap(message, "dp", 4)]
    acc0, chosen0, stat0, held = stats([message], [], items, at, True)

    message, own[1], own[2], stat0 = together(message, own[1], own[2], stat0)
    straight[1] = swap(message, "dp", 2)
    for j in range(3, n_shard):
        own.append(swap(own[j ^ top(j)], "shard", top(j)))
    acc1, chosen1, stat1 = stats(own[1:3], [stat0], held, at, False)

    message, straight[2], stat1, *own[3:] = together(message, straight[2], stat1, *own[3:])
    straight += [swap(message, "dp", 2 * k) for k in range(3, n_chips)]
    far = {2: [straight[2]] + [swap(straight[2], "shard", j) for j in (1, 2)]}
    acc2, chosen2, stat = stats(own[3:], [stat1], held, at, False)

    all_stats = [stat]
    bit = 1
    while bit < n_shard:
        got = swap(jnp.stack(all_stats) if bit > 1 else stat, "shard", bit)
        all_stats += [got[j] for j in range(bit)] if bit > 1 else [got]
        bit *= 2
    all_stats[-1], far[2][1], far[2][2], straight[1], *straight[3:] = together(
        all_stats[-1], far[2][1], far[2][2], straight[1], *straight[3:]
    )
    loss, sent, even, odd = dq_shares(all_stats, [acc0, acc1, acc2], [chosen0, chosen1, chosen2])

    for k in range(3, n_chips):
        far[k] = [straight[k]] + [swap(straight[k], "shard", j) for j in (1, 2)]
    for j in range(3, n_shard):
        far[2].append(swap(far[2][j ^ top(j)], "shard", top(j)))
    grads, token, chip_items, odd = item_grads([(own, 0)], [sent], items, None, span_rows, at, False, through=[odd])
    near = [straight[1], swap(own[1], "dp", 2)]
    early = [token, near[1], *[m for k in range(3, n_chips) for m in far[k][1:]]]
    terms = [sent]
    bit = 1
    while bit < n_chips:
        got = swap(jnp.stack(terms) + none(*early) if bit > 1 else sent, "dp", 2 * bit)
        terms += [got[j] for j in range(bit)] if bit > 1 else [got]
        bit *= 2
    near += [swap(own[j] + none(terms[n_chips - 1]), "dp", 2) for j in range(2, n_shard)]
    for k in range(3, n_chips):
        for j in range(3, n_shard):
            far[k].append(swap(far[k][j ^ top(j)], "shard", top(j)))
    grads, token = item_grads([(far[2], 0)], [terms[2]], chip_items, grads, span_rows, at, False)[:2]

    shares = even + swap(odd, "shard", 1) + none(token)
    half_way = shares
    bit = 2
    while bit < n_shard:
        shares = shares[0::2] + swap(shares[1::2], "shard", bit)
        bit *= 2
    query_grad = shares[0]
    for k in range(3, n_chips - 1):
        grads = item_grads([(far[k], 0)], [terms[k]], chip_items, grads, span_rows, at, False)[0]
    k = n_chips - 1
    most = [(far[k], 0), (near[: n_shard - 1], 0)]
    grads = item_grads(most, [terms[k], terms[1]], chip_items, grads, span_rows, at, False, [half_way])[0]
    rest = [(near[n_shard - 1 :], n_shard - 1)]
    mine, other = item_grads(rest, [terms[1]], chip_items, grads, span_rows, at, True, [query_grad])[2:]
    item_grad = mine + swap(other, "dp", 1)
    return loss.reshape(rows), query_grad, item_grad


def solution(mesh):
    placed = (
        P(("dp", "shard"), None),
        P("shard", None),
        P(("dp", "shard")),
        P(("dp", "shard"), None, None),
        P(("dp", "shard"), None),
    )
    return jax.shard_map(
        local,
        mesh=mesh,
        in_specs=placed,
        out_specs=(P(("dp", "shard")), P(("dp", "shard"), None), P(("shard", "dp"), None)),
        check_vma=False,
    )
```

```python
import functools

import jax
import jax.numpy as jnp
from jax import lax
from jax.experimental import pallas as pl
from jax.experimental.pallas import tpu as pltpu
from jax.sharding import PartitionSpec as P

TILE = 512
KMAX = 3
EXTRA = 8
LOADS = 8
GATHER = 8
STEP = 4
STAT = 4
MIB = 1024 * 1024
VMEM_LIMIT = 10 * MIB

very_low = -1e30
high, highest = lax.Precision.HIGH, lax.Precision.HIGHEST

smem = pl.BlockSpec(memory_space=pltpu.SMEM)
vmem = pl.BlockSpec(memory_space=pltpu.VMEM)
anywhere = pl.BlockSpec(memory_space=pl.ANY)
hbm = pl.BlockSpec(memory_space=pltpu.HBM)


def dot(a, b, dims=((1,), (0,)), precision=high):
    return lax.dot_general(a, b, (dims, ((), ())), precision=precision, preferred_element_type=jnp.float32)


def halves(x):
    upper = x.astype(jnp.bfloat16)
    return upper, (x - upper.astype(jnp.float32)).astype(jnp.bfloat16)


def dot3(a, b, dims=((1,), (0,))):
    def one(i, j):
        return lax.dot_general(a[i], b[j], (dims, ((), ())), preferred_element_type=jnp.float32)

    return (one(0, 1) + one(1, 0)) + one(0, 0)


def cost(us):
    return pl.CostEstimate(flops=0, bytes_accessed=int(us * 3.0e6), transcendentals=0)


def pack_kernel(step, ids_ref, counts_ref, q_ref, pos_ref, out_ref, sem):
    rows, width = q_ref.shape
    get_q = pltpu.make_async_copy(q_ref, out_ref.at[:rows], sem)
    get_q.start()
    out_ref[rows : rows + EXTRA, :] = jnp.zeros((EXTRA, width), jnp.float32)
    row = pos_ref[...].astype(jnp.float32)
    col = jnp.broadcast_to(row, (8, rows)).T[:, 0:1]
    at_row = lax.broadcasted_iota(jnp.int32, (rows, rows), 1)
    at_col = lax.broadcasted_iota(jnp.int32, (rows, rows), 0)
    before = (row < col) | ((row == col) & (at_row < at_col))
    rank = jnp.sum(before.astype(jnp.float32), axis=1, keepdims=True)
    placed = rank == at_row.astype(jnp.float32)
    sorted_pos = jnp.sum(jnp.where(placed, col, 0.0), axis=0, keepdims=True)
    sorted_at = jnp.sum(jnp.where(placed, at_col.astype(jnp.float32), 0.0), axis=0, keepdims=True)
    starts = lax.broadcasted_iota(jnp.int32, (rows, width), 1).astype(jnp.float32) * step
    bounds = jnp.sum((col < starts).astype(jnp.float32), axis=0, keepdims=True)
    lane = lax.broadcasted_iota(jnp.int32, (1, width), 1)
    lists = jnp.zeros((1, width), jnp.int32)
    n = counts_ref.shape[1]
    for i in range(n * KMAX):
        lists = jnp.where(lane == i, ids_ref[0, i // KMAX, i % KMAX], lists)
    for i in range(n):
        lists = jnp.where(lane == n * KMAX + i, counts_ref[0, i], lists)
    per = rows // width
    out_ref[rows + 3 * per : rows + 3 * per + 1, :] = lists.astype(jnp.float32)
    out_ref[rows + 3 * per + 1 : rows + 3 * per + 2, :] = bounds
    for first, values in ((0, row), (per, sorted_pos), (2 * per, sorted_at)):
        for i in range(per):
            out_ref[rows + first + i : rows + first + i + 1, :] = values[:, i * width : (i + 1) * width]
    get_q.wait()


def pack(queries, positive, tile_ids, counts, step):
    rows, width = queries.shape
    return pl.pallas_call(
        functools.partial(pack_kernel, float(step)),
        out_shape=jax.ShapeDtypeStruct((rows + EXTRA, width), jnp.float32),
        in_specs=[smem, smem, hbm, vmem],
        out_specs=vmem,
        scratch_shapes=[pltpu.SemaphoreType.DMA],
        compiler_params=pltpu.CompilerParams(vmem_limit_bytes=VMEM_LIMIT),
        cost_estimate=cost(2),
        name="pack",
    )(tile_ids, counts, queries, positive.reshape(1, rows))


class Lists:
    def __init__(self, ref, rows, shard_at, n_shard):
        self.ref, self.rows, self.shard_at, self.n_shard = ref, rows, shard_at, n_shard
        self.width = ref.shape[2]
        self.per = rows // self.width
        self.shift = self.width.bit_length() - 1

    def entry(self, b, first, i):
        return self.ref[b, first + (i >> self.shift), i & (self.width - 1)]

    def sorted_pos(self, b, i):
        return self.entry(b, self.per, i)

    def place(self, b, i):
        return self.entry(b, 2 * self.per, i)

    def tile(self, b, k):
        return self.ref[b, 3 * self.per, self.shard_at * KMAX + k]

    def count(self, b):
        return self.ref[b, 3 * self.per, self.n_shard * KMAX + self.shard_at]

    def bound(self, b, i):
        return self.ref[b, 3 * self.per + 1, i]


def swap(x, axis, bits):
    return lax.ppermute(x, axis, [(i, i ^ bits) for i in range(lax.axis_size(axis))])


def none(*xs):
    return sum(jnp.minimum(jnp.abs(x[(0,) * x.ndim]), 0.0) for x in xs)


def together(*xs):
    return lax.optimization_barrier(xs)


def stats_kernel(n, n_before, n_shard, loads, at, *refs):
    msgs, refs = refs[:n], refs[n:]
    befores, refs = refs[:n_before], refs[n_before:]
    source, acc_ref, chosen_ref, stat_ref, refs = refs[0], refs[1], refs[2], refs[3], refs[4:]
    items = source
    if loads:
        items, refs = refs[0], refs[1:]
    if loads:
        tiles, tile_sems, refs = refs[0], refs[1], refs[2:]
    q_ref, rowbuf, whole, lists_ref, sems, load_sems = refs
    rows = q_ref.shape[1] - EXTRA
    width = q_ref.shape[2]
    per = rows // width
    lists = Lists(lists_ref, rows, at[0], n_shard)
    base, local_rows = at[1], items.shape[0]
    chunk = local_rows // LOADS
    get_lists = pltpu.make_async_copy(whole, lists_ref, sems.at[1, 0])

    def get_q(j):
        return pltpu.make_async_copy(msgs[j], q_ref.at[j], sems.at[0, j])

    def get_items(i):
        part = pl.ds(i * chunk, chunk)
        return pltpu.make_async_copy(source.at[part], items.at[part], load_sems.at[i])

    def get_tile(k):
        start = pl.multiple_of(lists.tile(0, k) * TILE, TILE)
        return pltpu.make_async_copy(source.at[pl.ds(start, TILE)], tiles.at[k], tile_sems.at[k])

    for j in range(n):
        get_q(j).start()
    first = 0
    for before in befores:
        stat_ref[first : first + before.shape[0]] = before[...]
        first += before.shape[0]
    for j in range(n):
        get_q(j).wait()
    whole[...] = q_ref[:, rows:, :].astype(jnp.int32)
    get_lists.start()
    get_lists.wait()
    if loads:

        @pl.loop(0, lists.count(0))
        def _(k):
            get_tile(k).start()

        for i in range(LOADS):
            get_items(i).start()

    @pl.loop(0, n)
    def _(b):
        q_t = q_ref[b, :rows, :].T
        q_halves = halves(q_t)
        acc_ref[b] = jnp.zeros(acc_ref.shape[1:], jnp.float32)

        def visit(k, carry):
            top, total = carry
            if loads:
                get_tile(k).wait()
                tile = tiles[k]
            else:
                tile = items[pl.ds(pl.multiple_of(lists.tile(b, k) * TILE, TILE), TILE), :]
            logits = dot3(halves(tile), q_halves)
            new_top = jnp.maximum(top, jnp.max(logits, axis=0, keepdims=True))
            prob = jnp.exp(logits - new_top)
            scale = jnp.exp(top - new_top)
            total = total * scale + jnp.sum(prob, axis=0, keepdims=True)
            acc_ref[b] = acc_ref[b] * scale + dot(tile.T, prob)
            return new_top, total

        start = (jnp.full((1, rows), very_low, jnp.float32), jnp.zeros((1, rows), jnp.float32))
        top, total = lax.fori_loop(0, lists.count(b), visit, start)

        if loads:
            for i in range(LOADS):
                get_items(i).wait()
        rowbuf[...] = jnp.zeros(rowbuf.shape, jnp.float32)
        low, high_end = lists.bound(b, at[0] * at[4]), lists.bound(b, (at[0] + 1) * at[4])

        @pl.loop(0, (high_end - low + GATHER - 1) // GATHER)
        def _(c):
            entries = [jnp.minimum(low + c * GATHER + u, high_end - 1) for u in range(GATHER)]
            got = [items[pl.ds(lists.sorted_pos(b, i) - base, 1), :] for i in entries]
            for i, row in zip(entries, got):
                rowbuf[pl.ds(lists.place(b, i), 1), :] = row

        chosen = rowbuf[...].T
        chosen_ref[b] = chosen
        pos = jnp.concatenate([q_ref[b, rows + i : rows + i + 1, :] for i in range(per)], axis=1).astype(jnp.int32)
        offset = pos - base
        inside = (offset >= 0) & (offset < local_rows)
        plogit = jnp.sum(q_t * chosen, axis=0, keepdims=True)
        new_top = jnp.maximum(top, jnp.where(inside, plogit, very_low))
        total = total * jnp.exp(top - new_top) + jnp.where(inside, jnp.exp(plogit - new_top), 0.0)
        stat_ref[first + b, 0:1, :] = top
        stat_ref[first + b, 1:2, :] = new_top + jnp.log(total)
        stat_ref[first + b, 2:3, :] = jnp.where(inside, plogit, 0.0)
        stat_ref[first + b, 3:4, :] = jnp.where(inside, 1.0, 0.0)


def stats(messages, befores, items, at, loads):
    n = len(messages)
    rows, width = messages[0].shape[0] - EXTRA, messages[0].shape[1]
    total = n + sum(b.shape[0] for b in befores)
    sums = jax.ShapeDtypeStruct((n, width, rows), jnp.float32)
    held = [pltpu.VMEM(items.shape, jnp.float32)] if loads else []
    return pl.pallas_call(
        functools.partial(stats_kernel, n, len(befores), lax.axis_size("shard"), loads),
        out_shape=(sums, sums, jax.ShapeDtypeStruct((total, STAT, rows), jnp.float32), *held),
        in_specs=[smem] + [anywhere] * n + [vmem] * len(befores) + [hbm if loads else vmem],
        out_specs=(vmem, vmem, vmem, *[vmem] * len(held)),
        scratch_shapes=[
            *([pltpu.VMEM((KMAX, TILE, width), jnp.float32), pltpu.SemaphoreType.DMA((KMAX,))] if loads else []),
            pltpu.VMEM((n, rows + EXTRA, width), jnp.float32),
            pltpu.VMEM((rows, width), jnp.float32),
            pltpu.VMEM((n, EXTRA, width), jnp.int32),
            pltpu.SMEM((n, EXTRA, width), jnp.int32),
            pltpu.SemaphoreType.DMA((2, n)),
            pltpu.SemaphoreType.DMA((LOADS,)),
        ],
        compiler_params=pltpu.CompilerParams(vmem_limit_bytes=VMEM_LIMIT),
        cost_estimate=cost(5 * n),
        name="stats",
    )(at, *messages, *befores, items)


def dq_kernel(n, counts, *refs):
    stat_refs, refs = refs[:n], refs[n:]
    acc_refs, refs = refs[: len(counts)], refs[len(counts) :]
    chosen_refs, refs = refs[: len(counts)], refs[len(counts) :]
    loss_ref, term_ref, even_ref, odd_ref = refs
    b = 0
    for acc_ref, chosen_ref, count in zip(acc_refs, chosen_refs, counts):
        for i in range(count):
            parts = [stat_refs[j][b ^ j, 1:2, :] for j in range(n)]
            top = functools.reduce(jnp.maximum, parts)
            lse = top + jnp.log(sum(jnp.exp(p - top) for p in parts))
            plogit = sum(stat_refs[j][b ^ j, 2:3, :] for j in range(n))
            weight = jnp.exp(plogit - lse) - 1.0
            term_ref[0, b : b + 1, :] = lse
            term_ref[1, b : b + 1, :] = weight
            if b == 0:
                loss_ref[...] = lse - plogit
            own = stat_refs[0]
            share = acc_ref[i] * jnp.exp(own[b, 0:1, :] - lse) + chosen_ref[i] * (weight * own[b, 3:4, :])
            (odd_ref if b % 2 else even_ref)[b // 2] = share.T
            b += 1


def dq_shares(all_stats, accs, chosens):
    n, _, rows = all_stats[0].shape
    width = accs[0].shape[1]
    share = jax.ShapeDtypeStruct((n // 2, rows, width), jnp.float32)
    return pl.pallas_call(
        functools.partial(dq_kernel, n, [a.shape[0] for a in accs]),
        out_shape=(jax.ShapeDtypeStruct((1, rows), jnp.float32), jax.ShapeDtypeStruct((2, n, rows), jnp.float32), share, share),
        compiler_params=pltpu.CompilerParams(vmem_limit_bytes=VMEM_LIMIT),
        cost_estimate=cost(3),
        name="dq",
    )(*all_stats, *accs, *chosens)


def item_kernel(groups, n_shard, n_waits, n_through, is_first, is_last, at, *refs):
    n = sum(size for size, _ in groups)
    weights, refs = refs[: len(groups)], refs[len(groups) :]
    msgs, refs = refs[:n], refs[n + n_waits :]
    lse_refs, refs = refs[: len(groups)], refs[len(groups) :]
    items, refs = refs[0], refs[1 if is_first else 2 :]
    acc, token, refs = refs[0], refs[1], refs[2:]
    if is_first:
        source, items, refs = items, refs[0], refs[1:]
    outs, refs = refs[: 2 * is_last], refs[2 * is_last + n_through :]
    q_ref, lse, whole, lists_ref, sems = refs
    rows, width = q_ref.shape[1] - EXTRA, q_ref.shape[2]
    span_rows = acc.shape[0]
    tiles = span_rows // TILE
    base, first_tile, core = at[1] + at[2] * TILE, at[2], at[3]
    chip = at[0] * at[4] + at[5]
    lists = Lists(lists_ref, rows, at[0], n_shard)
    get_lists = pltpu.make_async_copy(whole, lists_ref, sems.at[1, 0])

    def get_q(j):
        return pltpu.make_async_copy(msgs[j], q_ref.at[j], sems.at[0, j])

    for j in range(n):
        get_q(j).start()
    if is_first:
        start = pl.multiple_of(first_tile * TILE, TILE)
        get_items = pltpu.make_async_copy(source.at[pl.ds(start, span_rows)], items, sems.at[2, 0])
        get_items.start()
        acc[...] = jnp.zeros(acc.shape, jnp.float32)
    token[...] = jnp.zeros(token.shape, jnp.float32)
    for j in range(n):
        get_q(j).wait()
    whole[...] = q_ref[:, rows:, :].astype(jnp.int32)
    get_lists.start()
    get_lists.wait()

    def add_positives(b, weight, first):
        low, top = lists.bound(b, chip), lists.bound(b, chip + 1)

        @pl.loop(0, (top - low + STEP - 1) // STEP)
        def _(c):
            entries = [jnp.minimum(low + c * STEP + u, top - 1) for u in range(STEP)]
            rests = [jnp.where(low + c * STEP + u < top, 1.0, 0.0) for u in range(STEP)]
            heres = [lists.sorted_pos(b, i) - base for i in entries]
            places = [lists.place(b, i) for i in entries]
            olds = [acc[pl.ds(h, 1), :] for h in heres]
            terms = [q_ref[b, pl.ds(p, 1), :] * (weight[1, b - first, p] * r) for p, r in zip(places, rests)]
            for u in range(1, STEP):
                terms[u] = terms[u] + terms[u - 1] * jnp.where(heres[u] == heres[u - 1], 1.0, 0.0)
            for h, old, term in zip(heres, olds, terms):
                acc[pl.ds(h, 1), :] = old + term

    first = 0
    for (size, begin), weight, lse_ref in zip(groups, weights, lse_refs):
        lse[first : first + size, :] = lse_ref[0, begin : begin + size, :]
        pl.loop(first, first + size)(functools.partial(add_positives, weight=weight, first=first - begin))
        first += size

    if is_first:
        get_items.wait()

    @pl.loop(0, n)
    def _(b):
        @pl.loop(0, lists.count(b))
        def _(k):
            tile = lists.tile(b, k) - first_tile

            @pl.when((tile >= 0) & (tile < tiles))
            def _():
                here = pl.ds(pl.multiple_of(tile * TILE, TILE), TILE)
                q = q_ref[b, :rows, :]
                logits = dot3(halves(items[here, :]), halves(q), ((1,), (1,)))
                prob = jnp.exp(logits - lse[pl.ds(b, 1), :])
                acc[here, :] += dot(prob, q)

    if is_last:
        own = span_rows // 2
        mine, other = outs
        put = [
            pltpu.make_async_copy(acc.at[pl.ds(pl.multiple_of((1 - core) * own, 8), own)], other, sems.at[2, 0]),
            pltpu.make_async_copy(acc.at[pl.ds(pl.multiple_of(core * own, 8), own)], mine, sems.at[2, 1]),
        ]
        for p in put:
            p.start()
        for p in put:
            p.wait()


def item_grads(groups, terms, items, acc, span_rows, at, is_last, waits=(), through=()):
    waits = [*waits, *through]
    messages = [m for group, _ in groups for m in group]
    n = len(messages)
    rows, width = messages[0].shape[0] - EXTRA, messages[0].shape[1]
    is_first = acc is None
    half = jax.ShapeDtypeStruct((span_rows // 2, width), jnp.float32)
    chips = pltpu.VMEM((span_rows, width), jnp.float32)
    token = jax.ShapeDtypeStruct((1, 128), jnp.float32)
    more = [chips] if is_first else [half, half] if is_last else []
    carried = [] if is_first else [acc]
    sizes = [(len(group), begin) for group, begin in groups]
    return pl.pallas_call(
        functools.partial(item_kernel, sizes, lax.axis_size("shard"), len(waits), len(through), is_first, is_last),
        out_shape=(chips, token, *more, *[jax.ShapeDtypeStruct(x.shape, x.dtype) for x in through]),
        in_specs=[smem] * (1 + len(groups))
        + [anywhere] * (n + len(waits))
        + [vmem] * len(groups)
        + [hbm if is_first else vmem]
        + [vmem] * len(carried),
        out_specs=(vmem, vmem, *[vmem if is_first else anywhere] * len(more), *[anywhere] * len(through)),
        scratch_shapes=[
            pltpu.VMEM((n, rows + EXTRA, width), jnp.float32),
            pltpu.VMEM((n, rows), jnp.float32),
            pltpu.VMEM((n, EXTRA, width), jnp.int32),
            pltpu.SMEM((n, EXTRA, width), jnp.int32),
            pltpu.SemaphoreType.DMA((3, max(n, 2))),
        ],
        input_output_aliases={
            **({} if is_first else {2 + 2 * len(groups) + n + len(waits): 0}),
            **{1 + len(groups) + n + len(waits) - len(through) + i: 2 + len(more) + i for i in range(len(through))},
        },
        compiler_params=pltpu.CompilerParams(vmem_limit_bytes=VMEM_LIMIT + max(n - 4, 0) * MIB),
        cost_estimate=cost(2 * n),
        name="item_grads",
    )(at, *terms, *messages, *waits, *terms, items, *carried)


def local(queries, items, positive, tile_ids, counts):
    dp_at, shard_at = lax.axis_index("dp"), lax.axis_index("shard")
    n_dp, n_shard = lax.axis_size("dp"), lax.axis_size("shard")
    rows, width = queries.shape
    local_rows = items.shape[0]
    span_rows = 2 * (local_rows // n_dp)
    n_chips = n_dp // 2
    chip_at = dp_at // 2
    at = jnp.stack([shard_at, shard_at * local_rows, chip_at * (span_rows // TILE), dp_at % 2, n_chips, chip_at])
    at = at.astype(jnp.int32)

    def top(j):
        return 1 << (j.bit_length() - 1)

    items = pltpu.with_memory_space_constraint(items, pltpu.HBM)
    queries = pltpu.with_memory_space_constraint(queries, pltpu.HBM)
    message = pack(queries, positive, tile_ids, counts, span_rows)
    own = [message] + [swap(message, "shard", j) for j in (1, 2)]
    straight = [message, None, swap(message, "dp", 4)]
    acc0, chosen0, stat0, held = stats([message], [], items, at, True)

    message, own[1], own[2], stat0 = together(message, own[1], own[2], stat0)
    straight[1] = swap(message, "dp", 2)
    for j in range(3, n_shard):
        own.append(swap(own[j ^ top(j)], "shard", top(j)))
    acc1, chosen1, stat1 = stats(own[1:3], [stat0], held, at, False)

    message, straight[2], stat1, *own[3:] = together(message, straight[2], stat1, *own[3:])
    straight += [swap(message, "dp", 2 * k) for k in range(3, n_chips)]
    far = {2: [straight[2]] + [swap(straight[2], "shard", j) for j in (1, 2)]}
    acc2, chosen2, stat = stats(own[3:], [stat1], held, at, False)

    all_stats = [stat]
    bit = 1
    while bit < n_shard:
        got = swap(jnp.stack(all_stats) if bit > 1 else stat, "shard", bit)
        all_stats += [got[j] for j in range(bit)] if bit > 1 else [got]
        bit *= 2
    all_stats[-1], far[2][1], far[2][2], straight[1], *straight[3:] = together(
        all_stats[-1], far[2][1], far[2][2], straight[1], *straight[3:]
    )
    loss, sent, even, odd = dq_shares(all_stats, [acc0, acc1, acc2], [chosen0, chosen1, chosen2])

    for k in range(3, n_chips):
        far[k] = [straight[k]] + [swap(straight[k], "shard", j) for j in (1, 2)]
    for j in range(3, n_shard):
        far[2].append(swap(far[2][j ^ top(j)], "shard", top(j)))
    grads, token, chip_items, odd = item_grads([(own, 0)], [sent], items, None, span_rows, at, False, through=[odd])
    near = [straight[1], swap(own[1], "dp", 2)]
    early = [token, near[1], *[m for k in range(3, n_chips) for m in far[k][1:]]]
    terms = [sent]
    bit = 1
    while bit < n_chips:
        got = swap(jnp.stack(terms) + none(*early) if bit > 1 else sent, "dp", 2 * bit)
        terms += [got[j] for j in range(bit)] if bit > 1 else [got]
        bit *= 2
    near += [swap(own[j] + none(terms[n_chips - 1]), "dp", 2) for j in range(2, n_shard)]
    for k in range(3, n_chips):
        for j in range(3, n_shard):
            far[k].append(swap(far[k][j ^ top(j)], "shard", top(j)))
    grads, token = item_grads([(far[2], 0)], [terms[2]], chip_items, grads, span_rows, at, False)[:2]

    shares = even + swap(odd, "shard", 1)
    half_way = shares
    bit = 2
    while bit < n_shard:
        shares = shares[0::2] + swap(shares[1::2], "shard", bit)
        bit *= 2
    query_grad = shares[0]
    for k in range(3, n_chips - 1):
        grads = item_grads([(far[k], 0)], [terms[k]], chip_items, grads, span_rows, at, False)[0]
    k = n_chips - 1
    most = [(far[k], 0), (near[: n_shard - 1], 0)]
    grads = item_grads(most, [terms[k], terms[1]], chip_items, grads, span_rows, at, False, [half_way])[0]
    rest = [(near[n_shard - 1 :], n_shard - 1)]
    mine, other = item_grads(rest, [terms[1]], chip_items, grads, span_rows, at, True, [query_grad])[2:]
    item_grad = mine + swap(other, "dp", 1)
    return loss.reshape(rows), query_grad, item_grad


def solution(mesh):
    placed = (
        P(("dp", "shard"), None),
        P("shard", None),
        P(("dp", "shard")),
        P(("dp", "shard"), None, None),
        P(("dp", "shard"), None),
    )
    return jax.shard_map(
        local,
        mesh=mesh,
        in_specs=placed,
        out_specs=(P(("dp", "shard")), P(("dp", "shard"), None), P(("shard", "dp"), None)),
        check_vma=False,
    )
```
